32 devices in a mesh: groups: 2 (over x), gx: 16 (over z, y, core).
Axes of the slice: x: 2, y: 2, z: 4, core: 2. Of those that a mesh axis runs over, the one named last changes fastest.
Arguments:
- input_tiles: bfloat16 [16, 512, 1024], P('gx', 'groups'), parts along dimension 1, may hold values from -6 to 6
- grad_tiles: bfloat16 [16, 512, 1024], P('gx', 'groups'), parts along dimension 1, may hold values from -0.59765625 to 0.59765625
- context_tiles: bfloat16 [16, 128, 4096], P('gx', 'groups'), parts along dimension 1, may hold values from -6 to 6
- up_tiles: bfloat16 [16, 1024, 8192], P('gx'), may hold values from -0.0625 to 0.0625
- down_tiles: bfloat16 [16, 8192, 1024], P('gx'), may hold values from -0.046875 to 0.046875
- output_tiles: bfloat16 [16, 4096, 1024], P('gx'), may hold values from -0.0625 to 0.0625
Outputs:
- d_input: bfloat16 [16, 512, 1024], P('gx', 'groups'), parts along dimension 1
- d_context: bfloat16 [16, 128, 4096], P('gx', 'groups'), parts along dimension 1
- d_up: bfloat16 [16, 2048, 8192], P('gx', 'groups'), parts along dimension 1
- d_down: bfloat16 [16, 16384, 1024], P('gx', 'groups'), parts along dimension 1
- d_output: bfloat16 [16, 8192, 1024], P('gx', 'groups'), parts along dimension 1
The draws below stay inside these ranges and needn't reach their ends.
There are 2 independent parts, one for each index of `groups`. The reference program is written for one: setup_inputs(seed, part) draws one part's arguments, and reference() takes and returns one part's arrays. A program takes and returns all parts, laid end to end along the dimension named above; an argument that names none is the same for every part. Nothing has to cross between parts.
All inputs are finite; a program needn't handle non-finite values.
Results may differ from the reference program's by a relative error of at most 0.0052.
Values may be sent and summed in bfloat16 or wider, within the bound.
No kernel may reach another device: no remote copies, remote signals or barrier semaphores. Data moves between devices by JAX's collectives and lax.ppermute only.
A program may use at most 256 MiB of HBM per device.

```python
import jax
import jax.numpy as jnp

D = 8192
FF = 16384
TOKENS = 512
PGRID = 8
QGRID = 2
N_GX = 16


def block_levels(key, shape, shards, smallest, largest):
    def one(axis_at, shards_of):
        heights = jax.random.uniform(jax.random.fold_in(jax.random.fold_in(key, 6), axis_at), (shards_of,), jnp.float32, smallest / len(shards), largest / len(shards))
        return jnp.repeat(jnp.exp(heights), shape[axis_at] // shards_of).reshape((-1,) + (1,) * (len(shape) - axis_at - 1))

    gain = one(*shards[0])
    for cut in shards[1:]:
        gain = gain * one(*cut)
    return gain


def gaussian(own_key, extent, scale, most, cuts=(), dtype=jnp.bfloat16):
    array = scale * jax.random.normal(own_key, extent, jnp.float32)
    if cuts:
        array = array * block_levels(own_key, extent, cuts, -0.22, 0.18)
    return jnp.clip(array, -most, most).astype(dtype)


def setup_inputs(seed: int = 0, part: int = 0) -> dict:
    streams_of = jax.random.split(jax.random.key(seed), 7)
    part_keys = jax.random.split(jax.random.fold_in(streams_of[6], part), 7)
    input_tiles = gaussian(part_keys[0], (N_GX, TOKENS // QGRID, D // PGRID), 1.0, 6.0, ((0, 16),))
    grad_tiles = gaussian(part_keys[1], (N_GX, TOKENS // QGRID, D // PGRID), 0.1, 0.59765625, ((0, 16),))
    context_tiles = gaussian(part_keys[2], (N_GX, TOKENS // PGRID, D // QGRID), 1.0, 6.0, ((0, 16),))
    up_tiles = gaussian(streams_of[3], (N_GX, D // PGRID, FF // QGRID), D ** -0.5, 0.0625, ((0, 16),))
    down_tiles = gaussian(streams_of[4], (N_GX, FF // QGRID, D // PGRID), FF ** -0.5, 0.046875, ((0, 16),))
    output_tiles = gaussian(streams_of[5], (N_GX, D // QGRID, D // PGRID), D ** -0.5, 0.0625, ((0, 16),))
    return {"input_tiles": input_tiles, "grad_tiles": grad_tiles, "context_tiles": context_tiles, "up_tiles": up_tiles, "down_tiles": down_tiles, "output_tiles": output_tiles}


def gelu_tanh(value):
    return jax.nn.gelu(value, approximate=True)

def rows_by_q(tiles):
    count, rows, cols = tiles.shape
    grid = tiles.reshape(QGRID, PGRID, rows, cols)
    return grid.transpose(0, 2, 1, 3).reshape(QGRID * rows, PGRID * cols)

def rows_by_p(tiles):
    count, rows, cols = tiles.shape
    grid = tiles.reshape(QGRID, PGRID, rows, cols)
    return grid.transpose(1, 2, 0, 3).reshape(PGRID * rows, QGRID * cols)

def split_rows_q(full, rows, cols):
    grid = full.reshape(QGRID, rows, PGRID, cols)
    return grid.transpose(0, 2, 1, 3).reshape(QGRID * PGRID, rows, cols)

def split_rows_p(full, rows, cols):
    grid = full.reshape(PGRID, rows, QGRID, cols)
    return grid.transpose(2, 0, 1, 3).reshape(QGRID * PGRID, rows, cols)

def reference(input_tiles, grad_tiles, context_tiles, up_tiles, down_tiles, output_tiles):
    inputs = rows_by_q(input_tiles)
    grads = rows_by_q(grad_tiles)
    context = rows_by_p(context_tiles)
    up_full = rows_by_p(up_tiles)
    down_full = rows_by_q(down_tiles)
    proj_full = rows_by_q(output_tiles)
    pre_act = jnp.dot(inputs, up_full, preferred_element_type=jnp.float32)
    act, gelu_back = jax.vjp(gelu_tanh, pre_act)
    act = act.astype(jnp.bfloat16)
    hidden_grad = jnp.dot(grads, down_full.T, preferred_element_type=jnp.float32)
    d_pre = gelu_back(hidden_grad)[0].astype(jnp.bfloat16)
    d_down = jnp.dot(act.T, grads, preferred_element_type=jnp.float32).astype(jnp.bfloat16)
    d_up = jnp.dot(inputs.T, d_pre, preferred_element_type=jnp.float32).astype(jnp.bfloat16)
    d_input = (grads.astype(jnp.float32) + jnp.dot(d_pre, up_full.T, preferred_element_type=jnp.float32)).astype(jnp.bfloat16)
    d_output = jnp.dot(context.T, d_input, preferred_element_type=jnp.float32).astype(jnp.bfloat16)
    d_context = jnp.dot(d_input, proj_full.T, preferred_element_type=jnp.float32).astype(jnp.bfloat16)
    return (split_rows_q(d_input, TOKENS // QGRID, D // PGRID), split_rows_p(d_context, TOKENS // PGRID, D // QGRID), split_rows_p(d_up, D // PGRID, FF // QGRID), split_rows_q(d_down, FF // QGRID, D // PGRID), split_rows_q(d_output, D // QGRID, D // PGRID))
```

```python
import jax
import jax.numpy as jnp
from jax import lax
from jax.sharding import PartitionSpec as P

CORE, NEAR, FAR = 1, 2, 4
SHARES = 8
GROUP = 16


def swap(value, mask):
    count = lax.axis_size("gx")
    return lax.ppermute(value, "gx", [(at, at ^ mask) for at in range(count)])


def gelu_tanh(value):
    return jax.nn.gelu(value, approximate=True)


def contract(left, right, left_dim, right_dim):
    return lax.dot_general(
        left, right, (((left_dim,), (right_dim,)), ((), ())), preferred_element_type=jnp.float32
    )


def gather(value, masks):
    for mask in masks:
        value = jnp.concatenate([value, swap(value, mask)], axis=0)
    return value


def scatter(value, masks):
    for mask in masks:
        half = value.shape[0] // 2
        sent = value[half:].astype(jnp.bfloat16)
        value = value[:half].astype(jnp.float32) + swap(sent, mask).astype(jnp.float32)
    return value


NEAR_FAR = (CORE, NEAR, FAR)
FAR_NEAR = (CORE, FAR, NEAR)


def offset_of(place, order):
    total = jnp.zeros_like(place)
    for at, mask in enumerate(order):
        total = total + mask * ((place >> (2 - at)) & 1)
    return total


def place_of(offset, order):
    total = jnp.zeros_like(offset)
    for at, mask in enumerate(order):
        total = total + jnp.where((offset & mask) != 0, 1 << (2 - at), 0)
    return total


def picked(source, value):
    columns = lax.broadcasted_iota(jnp.int32, (source.shape[0], value.shape[0]), 1)
    chooser = (source[:, None] == columns).astype(jnp.bfloat16)
    return contract(chooser, value, 1, 0).astype(jnp.bfloat16)


def body(input_tiles, grad_tiles, context_tiles, up_tiles, down_tiles, output_tiles):
    grid_index = lax.axis_index("gx")
    total_bits = lax.axis_size("gx").bit_length() - 1
    q_masks = [1 << bit for bit in range(3, total_bits)]
    own_p = grid_index & (SHARES - 1)
    own_q = grid_index >> 3
    inputs = input_tiles[0]
    grads = grad_tiles[0]
    context = context_tiles[0]
    up_block = up_tiles[0]
    down_block = down_tiles[0]
    proj_block = output_tiles[0]
    rows = inputs.shape[0]
    half_rows = rows // 2
    share_rows = half_rows // SHARES
    block_rows = context.shape[0]
    half_block = block_rows // 2
    q_count = 1 << len(q_masks)

    def half_source(order):
        at = jnp.arange(rows, dtype=jnp.int32)
        half, at = at // half_rows, at % half_rows
        share = own_p ^ offset_of(at // share_rows, order)
        inside = share * share_rows + at % share_rows
        return (inside // GROUP) * 2 * GROUP + half * GROUP + inside % GROUP

    def token_source(half, order):
        at = jnp.arange(SHARES * half_block, dtype=jnp.int32)
        block = own_p ^ offset_of(at // half_block, order)
        at = at % half_block
        token = block * block_rows + (at // GROUP) * 2 * GROUP + half * GROUP + at % GROUP
        local = token % rows
        inside = (local // (2 * GROUP)) * GROUP + local % GROUP
        place = place_of(own_p ^ (inside // share_rows), NEAR_FAR)
        return ((token // rows) ^ own_q) * half_rows + place * share_rows + inside % share_rows

    source_nf = half_source(NEAR_FAR)
    inputs_nf = picked(source_nf, inputs)
    grads_nf = picked(source_nf, grads)
    grads_fn = picked(half_source(FAR_NEAR), grads)

    def q_gather(value):
        value = value[None]
        for mask in q_masks:
            value = jnp.concatenate([value, swap(value, mask)], axis=0)
        return value

    chunks = {}
    for half in range(2):
        at = slice(half * half_rows, (half + 1) * half_rows)
        pair = q_gather(jnp.stack([inputs_nf[at], grads_fn[at]]))
        chunks["own", half] = pair[0, 0], pair[0, 1]
        chunks["other", half] = tuple(
            pair[1:, which].reshape((q_count - 1) * half_rows, -1) for which in range(2)
        )

    halves = context.reshape(block_rows // (2 * GROUP), 2, GROUP, -1)
    halves = [halves[:, half].reshape(half_block, -1) for half in range(2)]
    context_orders = (FAR_NEAR, NEAR_FAR)
    context_rows = [gather(halves[half], context_orders[half][::-1]) for half in range(2)]

    act_rows, dpre_rows, input_parts = {}, {}, {}

    def forward(name):
        chunk_in, chunk_grad = chunks[name]
        count = chunk_in.shape[0]
        pre_part = contract(chunk_in, up_block, 1, 0)
        hidden_part = contract(chunk_grad, down_block, 1, 1)
        pre_share = scatter(pre_part, NEAR_FAR)
        hidden_share = scatter(hidden_part, FAR_NEAR)
        act_share, gelu_back = jax.vjp(gelu_tanh, pre_share)
        dpre_share = gelu_back(hidden_share)[0].astype(jnp.bfloat16)
        act_rows[name] = gather(act_share.astype(jnp.bfloat16), FAR_NEAR[::-1])
        dpre_rows[name] = gather(dpre_share, NEAR_FAR[::-1])
        input_parts[name] = contract(dpre_rows[name], up_block, 1, 1)

    d_input_own, d_input_rows, d_context_halves = [], [], []

    def finish(half):
        own = input_parts["own", half][None]
        other = input_parts["other", half].reshape(q_count - 1, half_rows, -1)
        parts = jnp.concatenate([own, other], axis=0) if q_count > 2 else None
        if q_count == 2:
            share = own[0] + swap(other[0].astype(jnp.bfloat16), q_masks[0]).astype(jnp.float32)
        else:
            share = scatter(parts, q_masks[::-1])[0]
        at = slice(half * half_rows, (half + 1) * half_rows)
        d_input = (grads_nf[at].astype(jnp.float32) + share).astype(jnp.bfloat16)
        d_input_own.append(d_input)
        gathered = q_gather(d_input).reshape(q_count * half_rows, -1)
        by_order = {
            order: picked(token_source(half, order), gathered) for order in (NEAR_FAR, FAR_NEAR)
        }
        d_input_rows.append(by_order[context_orders[half]])
        columns = proj_block.shape[0] // 2
        first = contract(by_order[NEAR_FAR], proj_block[:columns], 1, 1)
        second = contract(by_order[FAR_NEAR], proj_block[columns:], 1, 1)
        first = scatter(first, NEAR_FAR)
        second = scatter(second, FAR_NEAR)
        d_context_halves.append(
            jnp.concatenate([first, second], axis=1).astype(jnp.bfloat16)
        )

    order = [("own", 0), ("other", 0), ("other", 1), ("own", 1)]
    for name in order[:2]:
        forward(name)
    finish(0)
    for name in order[2:]:
        forward(name)
    finish(1)

    act_all = jnp.concatenate([act_rows[name] for name in order], axis=0)
    dpre_all = jnp.concatenate([dpre_rows[name] for name in order], axis=0)
    in_all = jnp.concatenate([chunks[name][0] for name in order], axis=0)
    grad_all = jnp.concatenate([chunks[name][1] for name in order], axis=0)
    d_down = contract(act_all, grad_all, 0, 0).astype(jnp.bfloat16)
    d_up = contract(in_all, dpre_all, 0, 0).astype(jnp.bfloat16)

    own_all = jnp.concatenate(d_input_own, axis=0)
    columns = lax.broadcasted_iota(jnp.int32, (rows, rows), 1)
    chooser = (source_nf[:, None] == columns).astype(jnp.bfloat16)
    d_input = contract(chooser, own_all, 0, 0).astype(jnp.bfloat16)

    context_all = jnp.concatenate(context_rows, axis=0)
    d_input_all = jnp.concatenate(d_input_rows, axis=0)
    d_output = contract(context_all, d_input_all, 0, 0).astype(jnp.bfloat16)

    split = [
        part.reshape(block_rows // (2 * GROUP), 1, GROUP, -1) for part in d_context_halves
    ]
    d_context = jnp.concatenate(split, axis=1).reshape(block_rows, -1)
    return (d_input[None], d_context[None], d_up[None], d_down[None], d_output[None])


def solution(mesh):
    return jax.shard_map(
        body,
        mesh=mesh,
        in_specs=(
            P("gx", "groups", None),
            P("gx", "groups", None),
            P("gx", "groups", None),
            P("gx", None, None),
            P("gx", None, None),
            P("gx", None, None),
        ),
        out_specs=(
            P("gx", "groups", None),
            P("gx", "groups", None),
            P("gx", "groups", None),
            P("gx", "groups", None),
            P("gx", "groups", None),
        ),
        check_vma=False,
    )
```

```python
import jax
import jax.numpy as jnp
from jax import lax
from jax.experimental import pallas as pl
from jax.experimental.pallas import tpu as pltpu
from jax.sharding import PartitionSpec as P

CORE, NEAR, FAR = 1, 2, 4
SHARES = 8
GROUP = 16


def swap(value, mask):
    count = lax.axis_size("gx")
    return lax.ppermute(value, "gx", [(at, at ^ mask) for at in range(count)])


def gelu_tanh(value):
    return jax.nn.gelu(value, approximate=True)


def contract(left, right, left_dim, right_dim):
    return lax.dot_general(
        left, right, (((left_dim,), (right_dim,)), ((), ())), preferred_element_type=jnp.float32
    )


def tie(values, after):
    return lax.optimization_barrier((values, after))[0]


def gather(value, masks):
    for mask in masks:
        value = jnp.concatenate([value, swap(value, mask)], axis=0)
    return value


def scatter(value, masks):
    for mask in masks:
        half = value.shape[0] // 2
        sent = value[half:].astype(jnp.bfloat16)
        value = value[:half].astype(jnp.float32) + swap(sent, mask).astype(jnp.float32)
    return value


NEAR_FAR = (CORE, NEAR, FAR)
FAR_NEAR = (CORE, FAR, NEAR)


def offset_of(place, order):
    total = jnp.zeros_like(place)
    for at, mask in enumerate(order):
        total = total + mask * ((place >> (2 - at)) & 1)
    return total


def place_of(offset, order):
    total = jnp.zeros_like(offset)
    for at, mask in enumerate(order):
        total = total + jnp.where((offset & mask) != 0, 1 << (2 - at), 0)
    return total


def picked(source, value):
    columns = lax.broadcasted_iota(jnp.int32, (source.shape[0], value.shape[0]), 1)
    chooser = (source[:, None] == columns).astype(jnp.bfloat16)
    return contract(chooser, value, 1, 0).astype(jnp.bfloat16)


def estimate():
    return pl.CostEstimate(flops=1, bytes_accessed=1, transcendentals=0)


def params():
    return pltpu.CompilerParams(
        dimension_semantics=("arbitrary",), vmem_limit_bytes=44 * 1024 * 1024
    )


def tile_of(size, most):
    return most if size % most == 0 else size


def whole_block(part):
    return pl.BlockSpec(part.shape, lambda at: (0,) * part.ndim)


def hidden_parts(rows_in, rows_grad, up_block, down_block):
    count, depth = rows_in.shape
    width = up_block.shape[1]
    tile = tile_of(width, 1024)
    half = count // 2

    def kernel(in_ref, grad_ref, up_ref, down_ref, keep_ref, send_ref):
        pre = jnp.dot(in_ref[...], up_ref[...], preferred_element_type=jnp.float32)
        keep_ref[0] = pre[:half]
        send_ref[0] = pre[half:].astype(jnp.bfloat16)
        hidden = contract(grad_ref[...], down_ref[...], 1, 1)
        keep_ref[1] = hidden[:half]
        send_ref[1] = hidden[half:].astype(jnp.bfloat16)

    results = (
        jax.ShapeDtypeStruct((2, half, width), jnp.float32),
        jax.ShapeDtypeStruct((2, half, width), jnp.bfloat16),
    )
    operands = (rows_in, rows_grad, up_block, down_block)
    return pl.pallas_call(
        kernel,
        grid=(width // tile,),
        in_specs=[
            whole_block(rows_in),
            whole_block(rows_grad),
            pl.BlockSpec((depth, tile), lambda at: (0, at)),
            pl.BlockSpec((tile, depth), lambda at: (at, 0)),
        ],
        out_specs=[pl.BlockSpec((2, half, tile), lambda at: (0, 0, at))] * 2,
        out_shape=results,
        compiler_params=params(),
        cost_estimate=estimate(),
        name="hidden_parts",
    )(*operands)


def joined(pieces):
    if pieces[0].shape[0] % 16:
        return [jnp.concatenate(pieces, axis=0)]
    return pieces


def input_part(pieces, up_block):
    pieces = joined(pieces)
    count = sum(piece.shape[0] for piece in pieces)
    depth, width = up_block.shape
    tile = tile_of(width, 1024)

    def kernel(*refs):
        up_ref, out_ref = refs[-2:]
        rows = jnp.concatenate([ref[...] for ref in refs[:-2]], axis=0)
        part = contract(rows, up_ref[...], 1, 1)

        @pl.when(pl.program_id(0) == 0)
        def _():
            out_ref[...] = part

        @pl.when(pl.program_id(0) != 0)
        def _():
            out_ref[...] += part

    result = jax.ShapeDtypeStruct((count, depth), jnp.float32)
    operands = (*pieces, up_block)
    return pl.pallas_call(
        kernel,
        grid=(width // tile,),
        in_specs=[pl.BlockSpec((part.shape[0], tile), lambda at: (0, at)) for part in operands],
        out_specs=whole_block(result),
        out_shape=result,
        compiler_params=params(),
        cost_estimate=estimate(),
        name="input_part",
    )(*operands)


def up_gradient(turned, pieces):
    pieces = joined(pieces)
    depth, count = turned.shape
    width = pieces[0].shape[1]
    tile = tile_of(width, 512)

    def kernel(turned_ref, *refs):
        rows = jnp.concatenate([ref[...] for ref in refs[:-2]], axis=0)
        refs[-1][...] = jnp.zeros_like(refs[-1])
        refs[-2][...] = jnp.dot(
            turned_ref[...], rows, preferred_element_type=jnp.float32
        ).astype(jnp.bfloat16)

    result = jax.ShapeDtypeStruct((depth, width), jnp.bfloat16)
    mark = jax.ShapeDtypeStruct((8, 128), jnp.float32)
    operands = (turned, *pieces)
    return pl.pallas_call(
        kernel,
        grid=(width // tile,),
        in_specs=[whole_block(turned)]
        + [pl.BlockSpec((piece.shape[0], tile), lambda at: (0, at)) for piece in pieces],
        out_specs=(pl.BlockSpec((depth, tile), lambda at: (0, at)), whole_block(mark)),
        out_shape=(result, mark),
        compiler_params=params(),
        cost_estimate=estimate(),
        name="up_gradient",
    )(*operands)


def down_gradient(pieces, rows_grad):
    pieces = joined(pieces)
    count, depth = rows_grad.shape
    width = pieces[0].shape[1]
    tile = tile_of(width, 512)

    def kernel(grad_ref, *refs):
        rows = jnp.concatenate([ref[...] for ref in refs[:-2]], axis=0)
        refs[-1][...] = jnp.zeros_like(refs[-1])
        refs[-2][...] = contract(rows, grad_ref[...], 0, 0).astype(jnp.bfloat16)

    result = jax.ShapeDtypeStruct((width, depth), jnp.bfloat16)
    mark = jax.ShapeDtypeStruct((8, 128), jnp.float32)
    operands = (rows_grad, *pieces)
    return pl.pallas_call(
        kernel,
        grid=(width // tile,),
        in_specs=[whole_block(rows_grad)]
        + [pl.BlockSpec((piece.shape[0], tile), lambda at: (0, at)) for piece in pieces],
        out_specs=(pl.BlockSpec((tile, depth), lambda at: (at, 0)), whole_block(mark)),
        out_shape=(result, mark),
        compiler_params=params(),
        cost_estimate=estimate(),
        name="down_gradient",
    )(*operands)


def body(input_tiles, grad_tiles, context_tiles, up_tiles, down_tiles, output_tiles):
    grid_index = lax.axis_index("gx")
    total_bits = lax.axis_size("gx").bit_length() - 1
    q_masks = [1 << bit for bit in range(3, total_bits)]
    own_p = grid_index & (SHARES - 1)
    own_q = grid_index >> 3
    inputs = input_tiles[0]
    grads = grad_tiles[0]
    context = context_tiles[0]
    up_block = up_tiles[0]
    down_block = down_tiles[0]
    proj_block = output_tiles[0]
    rows = inputs.shape[0]
    half_rows = rows // 2
    share_rows = half_rows // SHARES
    block_rows = context.shape[0]
    half_block = block_rows // 2
    q_count = 1 << len(q_masks)

    def half_source(order):
        at = jnp.arange(rows, dtype=jnp.int32)
        half, at = at // half_rows, at % half_rows
        share = own_p ^ offset_of(at // share_rows, order)
        inside = share * share_rows + at % share_rows
        return (inside // GROUP) * 2 * GROUP + half * GROUP + inside % GROUP

    def token_source(half, order):
        at = jnp.arange(SHARES * half_block, dtype=jnp.int32)
        block = own_p ^ offset_of(at // half_block, order)
        at = at % half_block
        token = block * block_rows + (at // GROUP) * 2 * GROUP + half * GROUP + at % GROUP
        local = token % rows
        inside = (local // (2 * GROUP)) * GROUP + local % GROUP
        place = place_of(own_p ^ (inside // share_rows), NEAR_FAR)
        return ((token // rows) ^ own_q) * half_rows + place * share_rows + inside % share_rows

    source_nf = half_source(NEAR_FAR)
    inputs_nf = picked(source_nf, inputs)
    grads_nf = picked(source_nf, grads)
    grads_fn = picked(half_source(FAR_NEAR), grads)

    def q_gather(value):
        value = value[None]
        for mask in q_masks:
            value = jnp.concatenate([value, swap(value, mask)], axis=0)
        return value

    chunks = {}
    pairs = []
    for half in range(2):
        at = slice(half * half_rows, (half + 1) * half_rows)
        pairs.append(q_gather(jnp.stack([inputs_nf[at], grads_fn[at]])))
        chunks["own", half] = inputs_nf[at], grads_fn[at]

    state = {}
    late = [()]

    def held(values):
        return tie(values, late[0])

    def sums(name):
        if name[0] == "other":
            pair = held(pairs[name[1]][1:])
            chunks[name] = tuple(
                pair[:, which].reshape((q_count - 1) * half_rows, -1) for which in range(2)
            )
        chunk_in, chunk_grad = held(chunks[name])
        keep, send = hidden_parts(chunk_in, chunk_grad, up_block, down_block)
        state[name] = keep, swap(send, CORE)
        late[0] = send

    def summed(parts, which, at):
        keep, recv, *more = parts
        total = keep[which, at] + recv[which, at].astype(jnp.float32)
        for part in more:
            total = total + part[which][at].astype(jnp.float32)
        return total

    def halved(parts, which):
        count = parts[-1][which].shape[0] // 2
        return summed(parts, which, slice(count, 2 * count)).astype(jnp.bfloat16)

    def sums_core(name):
        parts = held(state[name])
        send = halved(parts, 0), halved(parts, 1)
        state[name] = *parts, (swap(send[0], NEAR), swap(send[1], FAR))
        late[0] = send

    def sums_one(name):
        parts = held(state[name])
        send = halved(parts, 0), halved(parts, 1)
        state[name] = *parts, (swap(send[0], FAR), swap(send[1], NEAR))
        late[0] = send

    def gelu(name):
        parts = held(state[name])
        at = slice(0, parts[-1][0].shape[0])
        act, gelu_back = jax.vjp(gelu_tanh, summed(parts, 0, at))
        dpre = gelu_back(summed(parts, 1, at))[0].astype(jnp.bfloat16)
        act = act.astype(jnp.bfloat16)
        state[name] = dpre, act, swap(dpre, FAR), swap(act, NEAR)
        late[0] = dpre, act

    def spread_one(name):
        dpre, act, dpre_recv, act_recv = held(state[name])
        dpre = jnp.concatenate([dpre, dpre_recv], axis=0)
        act = jnp.concatenate([act, act_recv], axis=0)
        state[name] = swap(dpre, NEAR), swap(act, FAR)
        dpre_rows[name] = [dpre, swap(dpre, CORE)]
        act_rows[name] = [act, swap(act, CORE)]
        late[0] = dpre, act

    act_rows, dpre_rows, input_parts = {}, {}, {}

    def spread_two(name):
        dpre, act = held(state[name])
        first, far = dpre_rows[name]
        dpre_rows[name] = [first, dpre, far, swap(dpre, CORE)]
        first, far = act_rows[name]
        act_rows[name] = [first, act, far, swap(act, CORE)]
        late[0] = dpre, act

    q_state, d_input_own, d_input_rows, d_context_halves = {}, {}, {}, {}

    def back(name):
        dpre_rows[name] = held(dpre_rows[name])
        part = input_part(dpre_rows[name], up_block)
        input_parts[name] = part
        late[0] = part[:8, :128]
        if name[0] == "other" and q_count == 2:
            sent = part.astype(jnp.bfloat16)
            q_state[name[1]] = swap(sent, q_masks[0])
            late[0] = sent

    def own_rows(half):
        own = input_parts["own", half]
        if q_count == 2:
            own, recv = held((own, q_state[half]))
            share = own + recv.astype(jnp.float32)
        else:
            other = input_parts["other", half].reshape(q_count - 1, half_rows, -1)
            share = scatter(jnp.concatenate([own[None], other], axis=0), q_masks[::-1])[0]
        at = slice(half * half_rows, (half + 1) * half_rows)
        d_input = (grads_nf[at].astype(jnp.float32) + share).astype(jnp.bfloat16)
        d_input_own[half] = d_input
        q_state[half] = q_gather(d_input)
        late[0] = d_input

    context_orders = (FAR_NEAR, NEAR_FAR)

    def context_sums(half):
        gathered = held(q_state[half]).reshape(q_count * half_rows, -1)
        by_order = {
            order: picked(token_source(half, order), gathered) for order in (NEAR_FAR, FAR_NEAR)
        }
        d_input_rows[half] = by_order[context_orders[half]]
        columns = proj_block.shape[0] // 2
        first = contract(by_order[NEAR_FAR], proj_block[:columns], 1, 1)
        second = contract(by_order[FAR_NEAR], proj_block[columns:], 1, 1)
        at = first.shape[0] // 2
        sent = jnp.concatenate([first[at:], second[at:]], axis=1).astype(jnp.bfloat16)
        q_state[half] = (first, second), swap(sent, CORE)
        late[0] = sent

    def context_summed(parts, which, at):
        full, recv, *more = parts
        columns = full[which].shape[1]
        here = slice(which * columns, (which + 1) * columns)
        total = full[which][at] + recv[at, here].astype(jnp.float32)
        for part in more:
            total = total + part[which][at].astype(jnp.float32)
        return total

    def context_halved(parts, which, count):
        return context_summed(parts, which, slice(count, 2 * count)).astype(jnp.bfloat16)

    def context_core(half):
        parts = held(q_state[half])
        count = parts[1].shape[0] // 2
        sent = context_halved(parts, 0, count), context_halved(parts, 1, count)
        q_state[half] = *parts, (swap(sent[0], NEAR), swap(sent[1], FAR))
        late[0] = sent

    def context_one(half):
        parts = held(q_state[half])
        count = parts[1].shape[0] // 4
        sent = context_halved(parts, 0, count), context_halved(parts, 1, count)
        q_state[half] = *parts, (swap(sent[0], FAR), swap(sent[1], NEAR))
        late[0] = sent

    def context_two(half):
        parts = held(q_state[half])
        at = slice(0, parts[1].shape[0] // 4)
        first, second = context_summed(parts, 0, at), context_summed(parts, 1, at)
        d_context_halves[half] = jnp.concatenate([first, second], axis=1).astype(jnp.bfloat16)
        late[0] = d_context_halves[half]

    saved = {}

    def saved_start():
        halves = held(context).reshape(block_rows // (2 * GROUP), 2, GROUP, -1)
        halves = [halves[:, half].reshape(half_block, -1) for half in range(2)]
        saved["rows"] = halves
        saved["recv"] = swap(halves[0], NEAR), swap(halves[1], FAR)

    def saved_next(masks):
        halves, recv = held((saved["rows"], saved["recv"]))
        halves = [
            jnp.concatenate([mine, theirs], axis=0) for mine, theirs in zip(halves, recv)
        ]
        saved["rows"] = halves
        if masks:
            saved["recv"] = [swap(rows, mask) for rows, mask in zip(halves, masks)]
        late[0] = halves

    own0, other0, other1, own1 = ("own", 0), ("other", 0), ("other", 1), ("own", 1)
    order = [own0, other0, other1, own1]
    sums(own0)
    sums_core(own0)
    sums(own1)
    sums_one(own0)
    sums_core(own1)
    saved_start()
    sums(other0)
    gelu(own0)
    sums_one(own1)
    sums_core(other0)
    saved_next((FAR, NEAR))
    sums(other1)
    in_all = held(jnp.concatenate([chunks[name][0] for name in order], axis=0))
    turned = in_all.T
    grad_all = jnp.concatenate([chunks[name][1] for name in order], axis=0)
    late[0] = late[0], turned[:8, :128], grad_all[:8, :128]
    spread_one(own0)
    sums_one(other0)
    sums_core(other1)
    saved_next((CORE, CORE))
    spread_two(own0)
    gelu(other0)
    sums_one(other1)
    back(own0)
    saved_next(())
    spread_one(other0)
    gelu(other1)
    spread_two(other0)
    spread_one(other1)
    gelu(own1)
    back(other0)
    spread_two(other1)
    spread_one(own1)
    own_rows(0)
    back(other1)
    spread_two(own1)
    context_sums(0)
    context_core(0)
    back(own1)
    own_rows(1)
    context_one(0)
    pieces = held([piece for name in order for piece in dpre_rows[name]])
    d_up, late[0] = up_gradient(turned, pieces)
    context_sums(1)
    context_two(0)
    pieces = held([piece for name in order for piece in act_rows[name]])
    d_down, late[0] = down_gradient(pieces, grad_all)
    context_core(1)
    d_input_all = held(jnp.concatenate([d_input_rows[0], d_input_rows[1]], axis=0))
    context_all = jnp.concatenate(saved["rows"], axis=0)
    d_output = contract(context_all, d_input_all, 0, 0).astype(jnp.bfloat16)
    context_one(1)
    context_two(1)

    own_all = jnp.concatenate([d_input_own[0], d_input_own[1]], axis=0)
    columns = lax.broadcasted_iota(jnp.int32, (rows, rows), 1)
    chooser = (source_nf[:, None] == columns).astype(jnp.bfloat16)
    d_input = contract(chooser, own_all, 0, 0).astype(jnp.bfloat16)

    split = [
        d_context_halves[half].reshape(block_rows // (2 * GROUP), 1, GROUP, -1)
        for half in range(2)
    ]
    d_context = jnp.concatenate(split, axis=1).reshape(block_rows, -1)
    return (d_input[None], d_context[None], d_up[None], d_down[None], d_output[None])


def solution(mesh):
    return jax.shard_map(
        body,
        mesh=mesh,
        in_specs=(
            P("gx", "groups", None),
            P("gx", "groups", None),
            P("gx", "groups", None),
            P("gx", None, None),
            P("gx", None, None),
            P("gx", None, None),
        ),
        out_specs=(
            P("gx", "groups", None),
            P("gx", "groups", None),
            P("gx", "groups", None),
            P("gx", "groups", None),
            P("gx", "groups", None),
        ),
        check_vma=False,
    )
```

```python
import jax
import jax.numpy as jnp
from jax import lax
from jax.experimental import pallas as pl
from jax.experimental.pallas import tpu as pltpu
from jax.sharding import PartitionSpec as P

CORE, NEAR, FAR = 1, 2, 4
SHARES = 8
GROUP = 16


def swap(value, mask):
    count = lax.axis_size("gx")
    return lax.ppermute(value, "gx", [(at, at ^ mask) for at in range(count)])


def gelu_tanh(value):
    return jax.nn.gelu(value, approximate=True)


def contract(left, right, left_dim, right_dim):
    return lax.dot_general(
        left, right, (((left_dim,), (right_dim,)), ((), ())), preferred_element_type=jnp.float32
    )


def gather(value, masks):
    for mask in masks:
        value = jnp.concatenate([value, swap(value, mask)], axis=0)
    return value


def scatter(value, masks):
    for mask in masks:
        half = value.shape[0] // 2
        sent = value[half:].astype(jnp.bfloat16)
        value = value[:half].astype(jnp.float32) + swap(sent, mask).astype(jnp.float32)
    return value


NEAR_FAR = (CORE, NEAR, FAR)
FAR_NEAR = (CORE, FAR, NEAR)


def offset_of(place, order):
    total = jnp.zeros_like(place)
    for at, mask in enumerate(order):
        total = total + mask * ((place >> (2 - at)) & 1)
    return total


def place_of(offset, order):
    total = jnp.zeros_like(offset)
    for at, mask in enumerate(order):
        total = total + jnp.where((offset & mask) != 0, 1 << (2 - at), 0)
    return total


def picked(source, value):
    columns = lax.broadcasted_iota(jnp.int32, (source.shape[0], value.shape[0]), 1)
    chooser = (source[:, None] == columns).astype(jnp.bfloat16)
    return contract(chooser, value, 1, 0).astype(jnp.bfloat16)


def estimate():
    return pl.CostEstimate(flops=1, bytes_accessed=1, transcendentals=0)


def params():
    return pltpu.CompilerParams(
        dimension_semantics=("arbitrary",), vmem_limit_bytes=44 * 1024 * 1024
    )


def tile_of(size, most):
    return most if size % most == 0 else size


def whole_block(part):
    return pl.BlockSpec(part.shape, lambda at: (0,) * part.ndim)


def run(kernel, operands, in_specs, out_specs, out_shape, grid, name, marks, aliases=None):
    count = len(operands)

    def body_of(*refs):
        kernel(*refs[:count], *refs[count + len(marks) :])

    return pl.pallas_call(
        body_of,
        grid=grid,
        in_specs=list(in_specs) + [pl.BlockSpec(memory_space=pl.ANY)] * len(marks),
        out_specs=out_specs,
        out_shape=out_shape,
        input_output_aliases=aliases or {},
        compiler_params=params(),
        cost_estimate=estimate(),
        name=name,
    )(*operands, *marks)


def hidden_parts(rows_in, rows_grad, up_block, down_block, first, width, *, marks):
    count, depth = rows_in.shape
    tile = tile_of(width, 512)
    skip = first // tile
    half = count // 2

    def kernel(in_ref, grad_ref, up_ref, down_ref, keep_ref, send_ref):
        pre = jnp.dot(in_ref[...], up_ref[...], preferred_element_type=jnp.float32)
        keep_ref[0] = pre[:half]
        send_ref[0] = pre[half:].astype(jnp.bfloat16)
        hidden = contract(grad_ref[...], down_ref[...], 1, 1)
        keep_ref[1] = hidden[:half]
        send_ref[1] = hidden[half:].astype(jnp.bfloat16)

    return run(
        kernel,
        (rows_in, rows_grad, up_block, down_block),
        [
            whole_block(rows_in),
            whole_block(rows_grad),
            pl.BlockSpec((depth, tile), lambda at: (0, at + skip)),
            pl.BlockSpec((tile, depth), lambda at: (at + skip, 0)),
        ],
        [pl.BlockSpec((2, half, tile), lambda at: (0, 0, at))] * 2,
        (
            jax.ShapeDtypeStruct((2, half, width), jnp.float32),
            jax.ShapeDtypeStruct((2, half, width), jnp.bfloat16),
        ),
        (width // tile,),
        "hidden_parts",
        marks,
    )


def joined(pieces):
    if pieces[0].shape[0] % 16:
        return [jnp.concatenate(pieces, axis=0)]
    return pieces


def input_part(pieces, up_block, first, start=None, *, marks):
    pieces = joined(pieces)
    count = sum(piece.shape[0] for piece in pieces)
    depth = up_block.shape[0]
    width = pieces[0].shape[1]
    tile = tile_of(width, 512)
    skip = first // tile
    begin = [] if start is None else [start]

    def kernel(*refs):
        up_ref, out_ref = refs[len(pieces)], refs[-1]
        rows = jnp.concatenate([ref[...] for ref in refs[: len(pieces)]], axis=0)
        part = contract(rows, up_ref[...], 1, 1)

        @pl.when(pl.program_id(0) == 0)
        def _():
            out_ref[...] = part + refs[-2][...] if begin else part

        @pl.when(pl.program_id(0) != 0)
        def _():
            out_ref[...] += part

    result = jax.ShapeDtypeStruct((count, depth), jnp.float32)
    return run(
        kernel,
        (*pieces, up_block, *begin),
        [pl.BlockSpec((piece.shape[0], tile), lambda at: (0, at)) for piece in pieces]
        + [pl.BlockSpec((depth, tile), lambda at: (0, at + skip))]
        + [whole_block(part) for part in begin],
        whole_block(result),
        result,
        (width // tile,),
        "input_part",
        marks,
    )


def up_gradient(turned, pieces, first, full, before=None, *, marks):
    pieces = joined(pieces)
    depth = turned.shape[0]
    width = pieces[0].shape[1]
    tile = tile_of(width, 512)
    skip = first // tile
    begin = [] if before is None else [before]

    def kernel(turned_ref, *refs):
        rows = jnp.concatenate([ref[...] for ref in refs[: len(pieces)]], axis=0)
        refs[-1][...] = jnp.zeros_like(refs[-1])
        refs[-2][...] = jnp.dot(
            turned_ref[...], rows, preferred_element_type=jnp.float32
        ).astype(jnp.bfloat16)

    mark = jax.ShapeDtypeStruct((8, 128), jnp.float32)
    return run(
        kernel,
        (turned, *pieces, *begin),
        [whole_block(turned)]
        + [pl.BlockSpec((piece.shape[0], tile), lambda at: (0, at)) for piece in pieces]
        + [pl.BlockSpec(memory_space=pl.ANY)] * len(begin),
        (pl.BlockSpec((depth, tile), lambda at: (0, at + skip)), whole_block(mark)),
        (jax.ShapeDtypeStruct((depth, full), jnp.bfloat16), mark),
        (width // tile,),
        "up_gradient",
        marks,
        {1 + len(pieces): 0} if begin else {},
    )


def down_gradient(pieces, rows_grad, first, full, before=None, *, marks):
    pieces = joined(pieces)
    depth = rows_grad.shape[1]
    width = pieces[0].shape[1]
    tile = tile_of(width, 512)
    skip = first // tile
    begin = [] if before is None else [before]

    def kernel(grad_ref, *refs):
        rows = jnp.concatenate([ref[...] for ref in refs[: len(pieces)]], axis=0)
        refs[-1][...] = jnp.zeros_like(refs[-1])
        refs[-2][...] = contract(rows, grad_ref[...], 0, 0).astype(jnp.bfloat16)

    mark = jax.ShapeDtypeStruct((8, 128), jnp.float32)
    return run(
        kernel,
        (rows_grad, *pieces, *begin),
        [whole_block(rows_grad)]
        + [pl.BlockSpec((piece.shape[0], tile), lambda at: (0, at)) for piece in pieces]
        + [pl.BlockSpec(memory_space=pl.ANY)] * len(begin),
        (pl.BlockSpec((tile, depth), lambda at: (at + skip, 0)), whole_block(mark)),
        (jax.ShapeDtypeStruct((full, depth), jnp.bfloat16), mark),
        (width // tile,),
        "down_gradient",
        marks,
        {1 + len(pieces): 0} if begin else {},
    )


def context_parts(rows_by_order, proj_block, *, marks):
    _, count, depth = rows_by_order.shape
    width = proj_block.shape[0]
    tile = tile_of(width // 2, 1024)
    each = width // 2 // tile
    half = count // 2

    def kernel(rows_ref, proj_ref, keep_ref, send_ref):
        part = contract(rows_ref[0], proj_ref[...], 1, 1)
        keep_ref[...] = part[:half]
        send_ref[...] = part[half:].astype(jnp.bfloat16)

    return run(
        kernel,
        (rows_by_order, proj_block),
        [
            pl.BlockSpec((1, count, depth), lambda at: (at // each, 0, 0)),
            pl.BlockSpec((tile, depth), lambda at: (at, 0)),
        ],
        [pl.BlockSpec((half, tile), lambda at: (0, at))] * 2,
        (
            jax.ShapeDtypeStruct((half, width), jnp.float32),
            jax.ShapeDtypeStruct((half, width), jnp.bfloat16),
        ),
        (width // tile,),
        "context_parts",
        marks,
    )


def body(input_tiles, grad_tiles, context_tiles, up_tiles, down_tiles, output_tiles):
    grid_index = lax.axis_index("gx")
    total_bits = lax.axis_size("gx").bit_length() - 1
    q_masks = [1 << bit for bit in range(3, total_bits)]
    own_p = grid_index & (SHARES - 1)
    own_q = grid_index >> 3
    inputs = input_tiles[0]
    grads = grad_tiles[0]
    context = context_tiles[0]
    up_block = up_tiles[0]
    down_block = down_tiles[0]
    proj_block = output_tiles[0]
    rows = inputs.shape[0]
    half_rows = rows // 2
    share_rows = rows // SHARES
    block_rows = context.shape[0]
    half_block = block_rows // 2
    q_count = 1 << len(q_masks)
    width = up_block.shape[1]
    part_width = width // 2

    def row_source(order):
        at = jnp.arange(rows, dtype=jnp.int32)
        share = own_p ^ offset_of(at // share_rows, order)
        return share * share_rows + at % share_rows

    def half_source(half):
        at = jnp.arange(half_rows, dtype=jnp.int32)
        local = (at // GROUP) * 2 * GROUP + half * GROUP + at % GROUP
        place = place_of(own_p ^ (local // share_rows), NEAR_FAR)
        return place * share_rows + local % share_rows

    def token_source(half, order):
        at = jnp.arange(SHARES * half_block, dtype=jnp.int32)
        block = own_p ^ offset_of(at // half_block, order)
        at = at % half_block
        token = block * block_rows + (at // GROUP) * 2 * GROUP + half * GROUP + at % GROUP
        local = token % rows
        inside = (local // (2 * GROUP)) * GROUP + local % GROUP
        return ((token // rows) ^ own_q) * half_rows + inside

    def q_gather(value):
        value = value[None]
        for mask in q_masks:
            value = jnp.concatenate([value, swap(value, mask)], axis=0)
        return value

    source_nf = row_source(NEAR_FAR)
    own_rows = picked(source_nf, inputs), picked(row_source(FAR_NEAR), grads)
    count_gx = lax.axis_size("gx")
    pair = jnp.stack(own_rows)
    if q_count == 2:
        groups = [[at, at + SHARES] for at in range(SHARES)]
        pairs = lax.all_gather(pair, "gx", axis_index_groups=groups)
    else:
        pairs = q_gather(pair)
    groups = [[at + low for at in range(SHARES)] for low in range(0, count_gx, SHARES)]
    context_all = lax.all_gather(context, "gx", axis_index_groups=groups, tiled=True)
    chunks = {"own": own_rows}
    grads_nf = picked(source_nf, grads)

    state, saved = {}, {}
    act_rows, dpre_rows = {}, {}
    late, alive = [pair], []

    def held(values):
        part = late[0]
        part = part.reshape(-1, part.shape[-1])[:8, :128]
        values, after = lax.optimization_barrier((values, part))
        alive.append(after)
        return values

    def marks():
        used = list(alive)
        alive.clear()
        return used

    def fetch_other():
        pair = held(pairs)
        pair = jnp.where(own_q == 0, pair[1:], pair[:1]) if q_count == 2 else pair[1:]
        chunks["other"] = tuple(
            pair[:, which].reshape((q_count - 1) * rows, -1) for which in range(2)
        )
        late[0] = pair

    def sums(name):
        chunk_in, chunk_grad = held(chunks[name[0]])
        keep, send = hidden_parts(
            chunk_in, chunk_grad, up_block, down_block, name[1] * part_width, part_width,
            marks=marks(),
        )
        state[name] = keep, swap(send, CORE)
        late[0] = send

    def summed(parts, which, at):
        keep, recv, *more = parts
        total = keep[which, at] + recv[which, at].astype(jnp.float32)
        for part in more:
            total = total + part[which][at].astype(jnp.float32)
        return total

    def halved(parts, which):
        count = parts[-1][which].shape[0] // 2
        return summed(parts, which, slice(count, 2 * count)).astype(jnp.bfloat16)

    def sums_core(name):
        parts = held(state[name])
        send = halved(parts, 0), halved(parts, 1)
        state[name] = *parts, (swap(send[0], NEAR), swap(send[1], FAR))
        late[0] = send[0]

    def sums_one(name):
        parts = held(state[name])
        send = halved(parts, 0), halved(parts, 1)
        state[name] = *parts, (swap(send[0], FAR), swap(send[1], NEAR))
        late[0] = send[0]

    def gelu(name):
        parts = held(state[name])
        at = slice(0, parts[-1][0].shape[0])
        act, gelu_back = jax.vjp(gelu_tanh, summed(parts, 0, at))
        dpre = gelu_back(summed(parts, 1, at))[0].astype(jnp.bfloat16)
        act = act.astype(jnp.bfloat16)
        state[name] = dpre, act, swap(dpre, FAR), swap(act, NEAR)
        late[0] = dpre

    def spread_one(name):
        dpre, act, dpre_recv, act_recv = held(state[name])
        dpre = jnp.concatenate([dpre, dpre_recv], axis=0)
        act = jnp.concatenate([act, act_recv], axis=0)
        state[name] = dpre, act, swap(dpre, NEAR), swap(act, FAR)
        late[0] = dpre

    def spread_two(name):
        dpre, act, dpre_recv, act_recv = held(state[name])
        dpre_rows[name] = [dpre, dpre_recv, swap(dpre, CORE), swap(dpre_recv, CORE)]
        act_rows[name] = [act, act_recv]
        late[0] = dpre_recv

    def act_core(name):
        act_rows[name] = held(act_rows[name])
        act_rows[name] = act_rows[name] + [swap(part, CORE) for part in act_rows[name]]

    parts = {}

    def back(name):
        dpre_rows[name] = held(dpre_rows[name])
        part = input_part(
            dpre_rows[name], up_block, name[1] * part_width, parts.get(name[0]), marks=marks()
        )
        parts[name[0]] = part
        late[0] = part

    def q_sums():
        if q_count == 2:
            sent = held(parts["other"]).astype(jnp.bfloat16)
            parts["recv"] = swap(sent, q_masks[0])
            late[0] = sent

    halves, d_context_halves = {}, {}

    def finish_rows():
        if q_count == 2:
            own, recv = held((parts["own"], parts["recv"]))
            share = own + recv.astype(jnp.float32)
        else:
            other = parts["other"].reshape(q_count - 1, rows, -1)
            share = scatter(
                jnp.concatenate([parts["own"][None], other], axis=0), q_masks[::-1]
            )[0]
        d_input = (grads_nf.astype(jnp.float32) + share).astype(jnp.bfloat16)
        saved["d_input"] = d_input
        for half in range(2):
            halves[half] = q_gather(picked(half_source(half), d_input))
        late[0] = d_input

    def context_sums(half):
        gathered = held(halves[half]).reshape(q_count * half_rows, -1)
        by_order = [picked(token_source(half, order), gathered) for order in (NEAR_FAR, FAR_NEAR)]
        saved["d_input", half] = gathered
        keep, send = context_parts(jnp.stack(by_order), proj_block, marks=marks())
        halves[half] = keep, swap(send, CORE)
        late[0] = send

    def context_summed(parts, which, at):
        keep, recv, *more = parts
        columns = keep.shape[1] // 2
        here = slice(which * columns, (which + 1) * columns)
        total = keep[at, here] + recv[at, here].astype(jnp.float32)
        for part in more:
            total = total + part[which][at].astype(jnp.float32)
        return total

    def context_halved(parts, which, count):
        return context_summed(parts, which, slice(count, 2 * count)).astype(jnp.bfloat16)

    def context_core(half):
        parts = held(halves[half])
        count = parts[1].shape[0] // 2
        sent = context_halved(parts, 0, count), context_halved(parts, 1, count)
        halves[half] = *parts, (swap(sent[0], NEAR), swap(sent[1], FAR))
        late[0] = sent[0]

    def context_one(half):
        parts = held(halves[half])
        count = parts[1].shape[0] // 4
        sent = context_halved(parts, 0, count), context_halved(parts, 1, count)
        halves[half] = *parts, (swap(sent[0], FAR), swap(sent[1], NEAR))
        late[0] = sent[0]

    def context_two(half):
        parts = held(halves[half])
        at = slice(0, parts[1].shape[0] // 4)
        first, second = context_summed(parts, 0, at), context_summed(parts, 1, at)
        d_context_halves[half] = jnp.concatenate([first, second], axis=1).astype(jnp.bfloat16)
        late[0] = d_context_halves[half]

    mine_a, mine_b, other_a, other_b = ("own", 0), ("own", 1), ("other", 0), ("other", 1)
    sums(mine_a)
    sums_core(mine_a)
    sums(mine_b)
    sums_one(mine_a)
    gelu(mine_a)
    sums_core(mine_b)
    spread_one(mine_a)
    sums_one(mine_b)
    fetch_other()
    sums(other_a)
    spread_two(mine_a)
    sums_core(other_a)
    sums(other_b)
    sums_one(other_a)
    gelu(other_a)
    sums_core(other_b)
    back(mine_a)
    act_core(mine_a)
    spread_one(other_a)
    sums_one(other_b)
    gelu(other_b)
    in_all = jnp.concatenate([chunks[name][0] for name in ("own", "other")], axis=0)
    turned = in_all.T
    grad_all = jnp.concatenate([chunks[name][1] for name in ("own", "other")], axis=0)
    spread_two(other_a)
    spread_one(other_b)
    gelu(mine_b)
    back(other_a)
    spread_two(other_b)
    spread_one(mine_b)
    act_core(other_a)
    pieces = held([piece for name in (mine_a, other_a) for piece in dpre_rows[name]])
    d_up, late[0] = up_gradient(turned, pieces, 0, width, marks=marks())
    back(other_b)
    q_sums()
    spread_two(mine_b)
    act_core(other_b)
    pieces = held([piece for name in (mine_a, other_a) for piece in act_rows[name]])
    d_down, late[0] = down_gradient(pieces, grad_all, 0, width, marks=marks())
    back(mine_b)
    finish_rows()
    act_core(mine_b)
    pieces = held([piece for name in (mine_b, other_b) for piece in dpre_rows[name]])
    d_up, late[0] = up_gradient(turned, pieces, part_width, width, d_up, marks=marks())
    context_sums(0)
    context_core(0)
    context_sums(1)
    context_core(1)
    pieces = held([piece for name in (mine_b, other_b) for piece in act_rows[name]])
    d_down, late[0] = down_gradient(pieces, grad_all, part_width, width, d_down, marks=marks())
    context_one(0)
    context_one(1)
    tokens = jnp.arange(q_count * rows, dtype=jnp.int32)
    local = tokens % rows
    source = ((tokens // rows) ^ own_q) * half_rows + (local // (2 * GROUP)) * GROUP
    source = source + local % GROUP + ((local // GROUP) % 2) * q_count * half_rows
    both = held(jnp.concatenate([saved["d_input", 0], saved["d_input", 1]], axis=0))
    d_input_all = picked(source, both)
    d_output = contract(context_all, d_input_all, 0, 0).astype(jnp.bfloat16)
    context_two(0)
    context_two(1)

    columns = lax.broadcasted_iota(jnp.int32, (rows, rows), 1)
    chooser = (source_nf[:, None] == columns).astype(jnp.bfloat16)
    d_input = contract(chooser, saved["d_input"], 0, 0).astype(jnp.bfloat16)

    split = [
        d_context_halves[half].reshape(block_rows // (2 * GROUP), 1, GROUP, -1)
        for half in range(2)
    ]
    d_context = jnp.concatenate(split, axis=1).reshape(block_rows, -1)
    return (d_input[None], d_context[None], d_up[None], d_down[None], d_output[None])


def solution(mesh):
    return jax.shard_map(
        body,
        mesh=mesh,
        in_specs=(
            P("gx", "groups", None),
            P("gx", "groups", None),
            P("gx", "groups", None),
            P("gx", None, None),
            P("gx", None, None),
            P("gx", None, None),
        ),
        out_specs=(
            P("gx", "groups", None),
            P("gx", "groups", None),
            P("gx", "groups", None),
            P("gx", "groups", None),
            P("gx", "groups", None),
        ),
        check_vma=False,
    )
```

```python
import jax
import jax.numpy as jnp
from jax import lax
from jax.experimental import pallas as pl
from jax.experimental.pallas import tpu as pltpu
from jax.sharding import PartitionSpec as P

CORE, NEAR, FAR = 1, 2, 4
SHARES = 8
GROUP = 16


def swap(value, mask):
    count = lax.axis_size("gx")
    return lax.ppermute(value, "gx", [(at, at ^ mask) for at in range(count)])


def gelu_tanh(value):
    return jax.nn.gelu(value, approximate=True)


def contract(left, right, left_dim, right_dim):
    return lax.dot_general(
        left, right, (((left_dim,), (right_dim,)), ((), ())), preferred_element_type=jnp.float32
    )


def gather(value, masks):
    for mask in masks:
        value = jnp.concatenate([value, swap(value, mask)], axis=0)
    return value


def scatter(value, masks):
    for mask in masks:
        half = value.shape[0] // 2
        sent = value[half:].astype(jnp.bfloat16)
        value = value[:half].astype(jnp.float32) + swap(sent, mask).astype(jnp.float32)
    return value


NEAR_FAR = (CORE, NEAR, FAR)
FAR_NEAR = (CORE, FAR, NEAR)


def offset_of(place, order):
    total = jnp.zeros_like(place)
    for at, mask in enumerate(order):
        total = total + mask * ((place >> (2 - at)) & 1)
    return total


def place_of(offset, order):
    total = jnp.zeros_like(offset)
    for at, mask in enumerate(order):
        total = total + jnp.where((offset & mask) != 0, 1 << (2 - at), 0)
    return total


def picked(source, value):
    columns = lax.broadcasted_iota(jnp.int32, (source.shape[0], value.shape[0]), 1)
    chooser = (source[:, None] == columns).astype(jnp.bfloat16)
    return contract(chooser, value, 1, 0).astype(jnp.bfloat16)


def estimate():
    return pl.CostEstimate(flops=1, bytes_accessed=1, transcendentals=0)


def params():
    return pltpu.CompilerParams(
        dimension_semantics=("arbitrary",), vmem_limit_bytes=44 * 1024 * 1024
    )


def tile_of(size, most):
    return most if size % most == 0 else size


def whole_block(part):
    return pl.BlockSpec(part.shape, lambda at: (0,) * part.ndim)


def run(kernel, operands, in_specs, out_specs, out_shape, grid, name, marks, aliases=None):
    count = len(operands)

    def body_of(*refs):
        kernel(*refs[:count], *refs[count + len(marks) :])

    return pl.pallas_call(
        body_of,
        grid=grid,
        in_specs=list(in_specs) + [pl.BlockSpec(memory_space=pl.ANY)] * len(marks),
        out_specs=out_specs,
        out_shape=out_shape,
        input_output_aliases=aliases or {},
        compiler_params=params(),
        cost_estimate=estimate(),
        name=name,
    )(*operands, *marks)


def hidden_parts(rows_in, rows_grad, up_block, down_block, first, width, *, marks):
    count, depth = rows_in.shape
    tile = tile_of(width, 512)
    skip = first // tile
    half = count // 2

    def kernel(in_ref, grad_ref, up_ref, down_ref, keep_ref, send_ref):
        pre = jnp.dot(in_ref[...], up_ref[...], preferred_element_type=jnp.float32)
        keep_ref[0] = pre[:half]
        send_ref[0] = pre[half:].astype(jnp.bfloat16)
        hidden = contract(grad_ref[...], down_ref[...], 1, 1)
        keep_ref[1] = hidden[:half]
        send_ref[1] = hidden[half:].astype(jnp.bfloat16)

    return run(
        kernel,
        (rows_in, rows_grad, up_block, down_block),
        [
            whole_block(rows_in),
            whole_block(rows_grad),
            pl.BlockSpec((depth, tile), lambda at: (0, at + skip)),
            pl.BlockSpec((tile, depth), lambda at: (at + skip, 0)),
        ],
        [pl.BlockSpec((2, half, tile), lambda at: (0, 0, at))] * 2,
        (
            jax.ShapeDtypeStruct((2, half, width), jnp.float32),
            jax.ShapeDtypeStruct((2, half, width), jnp.bfloat16),
        ),
        (width // tile,),
        "hidden_parts",
        marks,
    )


def joined(pieces):
    if pieces[0].shape[0] % 16:
        return [jnp.concatenate(pieces, axis=0)]
    return pieces


def input_part(pieces, up_block, first, start=None, *, marks):
    pieces = joined(pieces)
    count = sum(piece.shape[0] for piece in pieces)
    depth = up_block.shape[0]
    width = pieces[0].shape[1]
    tile = tile_of(width, 512)
    skip = first // tile
    begin = [] if start is None else [start]

    def kernel(*refs):
        up_ref, out_ref = refs[len(pieces)], refs[-1]
        rows = jnp.concatenate([ref[...] for ref in refs[: len(pieces)]], axis=0)
        part = contract(rows, up_ref[...], 1, 1)

        @pl.when(pl.program_id(0) == 0)
        def _():
            out_ref[...] = part + refs[-2][...] if begin else part

        @pl.when(pl.program_id(0) != 0)
        def _():
            out_ref[...] += part

    result = jax.ShapeDtypeStruct((count, depth), jnp.float32)
    return run(
        kernel,
        (*pieces, up_block, *begin),
        [pl.BlockSpec((piece.shape[0], tile), lambda at: (0, at)) for piece in pieces]
        + [pl.BlockSpec((depth, tile), lambda at: (0, at + skip))]
        + [whole_block(part) for part in begin],
        whole_block(result),
        result,
        (width // tile,),
        "input_part",
        marks,
    )


def up_gradient(turned, pieces, first, full, before=None, *, marks):
    pieces = joined(pieces)
    depth = turned.shape[0]
    width = pieces[0].shape[1]
    tile = tile_of(width, 512)
    skip = first // tile
    begin = [] if before is None else [before]

    def kernel(turned_ref, *refs):
        rows = jnp.concatenate([ref[...] for ref in refs[: len(pieces)]], axis=0)
        refs[-1][...] = jnp.zeros_like(refs[-1])
        refs[-2][...] = jnp.dot(
            turned_ref[...], rows, preferred_element_type=jnp.float32
        ).astype(jnp.bfloat16)

    mark = jax.ShapeDtypeStruct((8, 128), jnp.float32)
    return run(
        kernel,
        (turned, *pieces, *begin),
        [whole_block(turned)]
        + [pl.BlockSpec((piece.shape[0], tile), lambda at: (0, at)) for piece in pieces]
        + [pl.BlockSpec(memory_space=pl.ANY)] * len(begin),
        (pl.BlockSpec((depth, tile), lambda at: (0, at + skip)), whole_block(mark)),
        (jax.ShapeDtypeStruct((depth, full), jnp.bfloat16), mark),
        (width // tile,),
        "up_gradient",
        marks,
        {1 + len(pieces): 0} if begin else {},
    )


def down_gradient(pieces, rows_grad, first, full, before=None, *, marks):
    pieces = joined(pieces)
    depth = rows_grad.shape[1]
    width = pieces[0].shape[1]
    tile = tile_of(width, 512)
    skip = first // tile
    begin = [] if before is None else [before]

    def kernel(grad_ref, *refs):
        rows = jnp.concatenate([ref[...] for ref in refs[: len(pieces)]], axis=0)
        refs[-1][...] = jnp.zeros_like(refs[-1])
        refs[-2][...] = contract(rows, grad_ref[...], 0, 0).astype(jnp.bfloat16)

    mark = jax.ShapeDtypeStruct((8, 128), jnp.float32)
    return run(
        kernel,
        (rows_grad, *pieces, *begin),
        [whole_block(rows_grad)]
        + [pl.BlockSpec((piece.shape[0], tile), lambda at: (0, at)) for piece in pieces]
        + [pl.BlockSpec(memory_space=pl.ANY)] * len(begin),
        (pl.BlockSpec((tile, depth), lambda at: (at + skip, 0)), whole_block(mark)),
        (jax.ShapeDtypeStruct((full, depth), jnp.bfloat16), mark),
        (width // tile,),
        "down_gradient",
        marks,
        {1 + len(pieces): 0} if begin else {},
    )


def context_parts(rows_by_order, proj_block, *, marks):
    _, count, depth = rows_by_order.shape
    width = proj_block.shape[0]
    tile = tile_of(width // 2, 1024)
    each = width // 2 // tile
    half = count // 2

    def kernel(rows_ref, proj_ref, keep_ref, send_ref):
        part = contract(rows_ref[0], proj_ref[...], 1, 1)
        keep_ref[...] = part[:half]
        send_ref[...] = part[half:].astype(jnp.bfloat16)

    return run(
        kernel,
        (rows_by_order, proj_block),
        [
            pl.BlockSpec((1, count, depth), lambda at: (at // each, 0, 0)),
            pl.BlockSpec((tile, depth), lambda at: (at, 0)),
        ],
        [pl.BlockSpec((half, tile), lambda at: (0, at))] * 2,
        (
            jax.ShapeDtypeStruct((half, width), jnp.float32),
            jax.ShapeDtypeStruct((half, width), jnp.bfloat16),
        ),
        (width // tile,),
        "context_parts",
        marks,
    )


def body(input_tiles, grad_tiles, context_tiles, up_tiles, down_tiles, output_tiles):
    grid_index = lax.axis_index("gx")
    total_bits = lax.axis_size("gx").bit_length() - 1
    q_masks = [1 << bit for bit in range(3, total_bits)]
    own_p = grid_index & (SHARES - 1)
    own_q = grid_index >> 3
    inputs = input_tiles[0]
    grads = grad_tiles[0]
    context = context_tiles[0]
    up_block = up_tiles[0]
    down_block = down_tiles[0]
    proj_block = output_tiles[0]
    rows = inputs.shape[0]
    half_rows = rows // 2
    share_rows = rows // SHARES
    block_rows = context.shape[0]
    half_block = block_rows // 2
    q_count = 1 << len(q_masks)
    width = up_block.shape[1]
    part_width = width // 2

    def row_source(order):
        at = jnp.arange(rows, dtype=jnp.int32)
        share = own_p ^ offset_of(at // share_rows, order)
        return share * share_rows + at % share_rows

    def half_source(half):
        at = jnp.arange(half_rows, dtype=jnp.int32)
        local = (at // GROUP) * 2 * GROUP + half * GROUP + at % GROUP
        place = place_of(own_p ^ (local // share_rows), NEAR_FAR)
        return place * share_rows + local % share_rows

    def token_source(half, order):
        at = jnp.arange(SHARES * half_block, dtype=jnp.int32)
        block = own_p ^ offset_of(at // half_block, order)
        at = at % half_block
        token = block * block_rows + (at // GROUP) * 2 * GROUP + half * GROUP + at % GROUP
        local = token % rows
        inside = (local // (2 * GROUP)) * GROUP + local % GROUP
        return ((token // rows) ^ own_q) * half_rows + inside

    def q_gather(value):
        value = value[None]
        for mask in q_masks:
            value = jnp.concatenate([value, swap(value, mask)], axis=0)
        return value

    source_nf = row_source(NEAR_FAR)
    own_rows = picked(source_nf, inputs), picked(row_source(FAR_NEAR), grads)
    pairs = [q_gather(part)[1:] for part in own_rows]
    groups = [
        [at + low for at in range(SHARES)] for low in range(0, lax.axis_size("gx"), SHARES)
    ]
    context_all = lax.all_gather(context, "gx", axis_index_groups=groups, tiled=True)
    chunks = {"own": own_rows}
    grads_nf = picked(source_nf, grads)

    state, saved = {}, {}
    act_rows, dpre_rows = {}, {}
    late, alive = [own_rows[1]], []

    def corner(part):
        return part.reshape(-1, part.shape[-1])[:8, :128]

    def held(values):
        values, after = lax.optimization_barrier((values, corner(late[0])))
        alive.append(after)
        return values

    def marks():
        used = [*alive, corner(late[0])]
        alive.clear()
        return used

    def fetch(which):
        pairs[which] = held(pairs[which])
        late[0] = pairs[which]
        if which == 1:
            chunks["other"] = tuple(part.reshape((q_count - 1) * rows, -1) for part in pairs)

    def sums(name):
        chunk_in, chunk_grad = chunks[name[0]]
        keep, send = hidden_parts(
            chunk_in, chunk_grad, up_block, down_block, name[1] * part_width, part_width,
            marks=marks(),
        )
        state[name] = keep, swap(send, CORE)
        late[0] = send

    def summed(parts, which, at):
        keep, recv, *more = parts
        total = keep[which, at] + recv[which, at].astype(jnp.float32)
        for part in more:
            total = total + part[which][at].astype(jnp.float32)
        return total

    def halved(parts, which):
        count = parts[-1][which].shape[0] // 2
        return summed(parts, which, slice(count, 2 * count)).astype(jnp.bfloat16)

    def sums_core(name):
        parts = held(state[name])
        send = halved(parts, 0), halved(parts, 1)
        state[name] = *parts, (swap(send[0], NEAR), swap(send[1], FAR))
        late[0] = send[0]

    def sums_one(name):
        parts = held(state[name])
        send = halved(parts, 0), halved(parts, 1)
        state[name] = *parts, (swap(send[0], FAR), swap(send[1], NEAR))
        late[0] = send[0]

    def gelu(name):
        parts = held(state[name])
        at = slice(0, parts[-1][0].shape[0])
        act, gelu_back = jax.vjp(gelu_tanh, summed(parts, 0, at))
        dpre = gelu_back(summed(parts, 1, at))[0].astype(jnp.bfloat16)
        act = act.astype(jnp.bfloat16)
        state[name] = dpre, act
        late[0] = dpre

    def spread(name):
        dpre, act = held(state[name])
        state[name] = dpre, act, swap(dpre, FAR), swap(act, NEAR)

    def spread_one(name):
        dpre, act, dpre_recv, act_recv = held(state[name])
        dpre = jnp.concatenate([dpre, dpre_recv], axis=0)
        act = jnp.concatenate([act, act_recv], axis=0)
        state[name] = dpre, act, swap(dpre, NEAR), swap(act, FAR)
        late[0] = dpre

    def spread_two(name):
        dpre, act, dpre_recv, act_recv = held(state[name])
        dpre_rows[name] = [dpre, dpre_recv, swap(dpre, CORE), swap(dpre_recv, CORE)]
        act_rows[name] = act, act_recv
        late[0] = dpre_recv

    def act_core(name):
        act = jnp.concatenate(held(act_rows[name]), axis=0)
        act_rows[name] = [act, swap(act, CORE)]
        late[0] = act

    parts = {}

    def back(name):
        part = input_part(
            dpre_rows[name], up_block, name[1] * part_width, parts.get(name[0]), marks=marks()
        )
        parts[name[0]] = part
        late[0] = part

    def q_sums():
        if q_count == 2:
            sent = held(parts["other"]).astype(jnp.bfloat16)
            parts["recv"] = swap(sent, q_masks[0])
            late[0] = sent

    halves, d_context_halves = {}, {}

    def finish_rows():
        if q_count == 2:
            own, recv = held((parts["own"], parts["recv"]))
            share = own + recv.astype(jnp.float32)
        else:
            other = parts["other"].reshape(q_count - 1, rows, -1)
            share = scatter(
                jnp.concatenate([parts["own"][None], other], axis=0), q_masks[::-1]
            )[0]
        d_input = (grads_nf.astype(jnp.float32) + share).astype(jnp.bfloat16)
        saved["d_input"] = d_input
        source = jnp.concatenate([half_source(0), half_source(1)])
        ordered = picked(source, d_input)
        for half in range(2):
            halves[half] = q_gather(ordered[half * half_rows : (half + 1) * half_rows])
        late[0] = ordered

    def context_sums(half):
        gathered = held(halves[half]).reshape(q_count * half_rows, -1)
        by_order = [picked(token_source(half, order), gathered) for order in (NEAR_FAR, FAR_NEAR)]
        saved["d_input", half] = gathered
        keep, send = context_parts(jnp.stack(by_order), proj_block, marks=marks())
        halves[half] = keep, swap(send, CORE)
        late[0] = send

    def context_summed(parts, which, at):
        keep, recv, *more = parts
        columns = keep.shape[1] // 2
        here = slice(which * columns, (which + 1) * columns)
        total = keep[at, here] + recv[at, here].astype(jnp.float32)
        for part in more:
            total = total + part[which][at].astype(jnp.float32)
        return total

    def context_halved(parts, which, count):
        return context_summed(parts, which, slice(count, 2 * count)).astype(jnp.bfloat16)

    def context_core(half):
        parts = held(halves[half])
        count = parts[1].shape[0] // 2
        sent = context_halved(parts, 0, count), context_halved(parts, 1, count)
        halves[half] = *parts, (swap(sent[0], NEAR), swap(sent[1], FAR))
        late[0] = sent[0]

    def context_one(half):
        parts = held(halves[half])
        count = parts[1].shape[0] // 4
        sent = context_halved(parts, 0, count), context_halved(parts, 1, count)
        halves[half] = *parts, (swap(sent[0], FAR), swap(sent[1], NEAR))
        late[0] = sent[0]

    def context_two(half):
        parts = held(halves[half])
        at = slice(0, parts[1].shape[0] // 4)
        first, second = context_summed(parts, 0, at), context_summed(parts, 1, at)
        d_context_halves[half] = jnp.concatenate([first, second], axis=1).astype(jnp.bfloat16)
        late[0] = d_context_halves[half]

    mine_a, mine_b, other_a, other_b = ("own", 0), ("own", 1), ("other", 0), ("other", 1)
    sums(mine_a)
    sums_core(mine_a)
    sums(mine_b)
    fetch(0)
    sums_one(mine_a)
    gelu(mine_a)
    spread(mine_a)
    sums_core(mine_b)
    fetch(1)
    sums(other_a)
    sums_one(mine_b)
    spread_one(mine_a)
    gelu(mine_b)
    sums_core(other_a)
    sums(other_b)
    spread_two(mine_a)
    sums_one(other_a)
    sums_core(other_b)
    back(mine_a)
    gelu(other_a)
    spread(other_a)
    sums_one(other_b)
    in_all = jnp.concatenate([chunks[name][0] for name in ("own", "other")], axis=0)
    turned = in_all.T
    grad_all = jnp.concatenate([chunks[name][1] for name in ("own", "other")], axis=0)
    spread_one(other_a)
    gelu(other_b)
    spread(other_b)
    spread_two(other_a)
    spread_one(other_b)
    back(other_a)
    act_core(mine_a)
    spread(mine_b)
    pieces = [piece for name in (mine_a, other_a) for piece in dpre_rows[name]]
    d_up, late[0] = up_gradient(turned, pieces, 0, width, marks=marks())
    spread_two(other_b)
    act_core(other_a)
    spread_one(mine_b)
    back(other_b)
    q_sums()
    pieces = [piece for name in (mine_a, other_a) for piece in act_rows[name]]
    d_down, late[0] = down_gradient(pieces, grad_all, 0, width, marks=marks())
    spread_two(mine_b)
    act_core(other_b)
    back(mine_b)
    act_core(mine_b)
    finish_rows()
    pieces = [piece for name in (mine_b, other_b) for piece in dpre_rows[name]]
    d_up, late[0] = up_gradient(turned, pieces, part_width, width, d_up, marks=marks())
    context_sums(0)
    context_sums(1)
    context_core(0)
    context_core(1)
    pieces = [piece for name in (mine_b, other_b) for piece in act_rows[name]]
    d_down, late[0] = down_gradient(pieces, grad_all, part_width, width, d_down, marks=marks())
    context_one(0)
    context_one(1)
    tokens = jnp.arange(q_count * rows, dtype=jnp.int32)
    local = tokens % rows
    source = ((tokens // rows) ^ own_q) * half_rows + (local // (2 * GROUP)) * GROUP
    source = source + local % GROUP + ((local // GROUP) % 2) * q_count * half_rows
    both = jnp.concatenate([saved["d_input", 0], saved["d_input", 1]], axis=0)
    d_input_all = picked(source, both)
    d_output, late[0] = down_gradient(
        [context_all], d_input_all, 0, context_all.shape[1], marks=marks()
    )
    context_two(0)
    context_two(1)

    columns = lax.broadcasted_iota(jnp.int32, (rows, rows), 1)
    chooser = (source_nf[:, None] == columns).astype(jnp.bfloat16)
    d_input = contract(chooser, saved["d_input"], 0, 0).astype(jnp.bfloat16)

    split = [
        d_context_halves[half].reshape(block_rows // (2 * GROUP), 1, GROUP, -1)
        for half in range(2)
    ]
    d_context = jnp.concatenate(split, axis=1).reshape(block_rows, -1)
    return (d_input[None], d_context[None], d_up[None], d_down[None], d_output[None])


def solution(mesh):
    return jax.shard_map(
        body,
        mesh=mesh,
        in_specs=(
            P("gx", "groups", None),
            P("gx", "groups", None),
            P("gx", "groups", None),
            P("gx", None, None),
            P("gx", None, None),
            P("gx", None, None),
        ),
        out_specs=(
            P("gx", "groups", None),
            P("gx", "groups", None),
            P("gx", "groups", None),
            P("gx", "groups", None),
            P("gx", "groups", None),
        ),
        check_vma=False,
    )
```

```python
import jax
import jax.numpy as jnp
from jax import lax
from jax.experimental import pallas as pl
from jax.experimental.pallas import tpu as pltpu
from jax.sharding import PartitionSpec as P

CORE, NEAR, FAR = 1, 2, 4
SHARES = 8
GROUP = 16


def swap(value, mask):
    count = lax.axis_size("gx")
    return lax.ppermute(value, "gx", [(at, at ^ mask) for at in range(count)])


def gelu_tanh(value):
    return jax.nn.gelu(value, approximate=True)


def contract(left, right, left_dim, right_dim):
    return lax.dot_general(
        left, right, (((left_dim,), (right_dim,)), ((), ())), preferred_element_type=jnp.float32
    )


def gather(value, masks):
    for mask in masks:
        value = jnp.concatenate([value, swap(value, mask)], axis=0)
    return value


def scatter(value, masks):
    for mask in masks:
        half = value.shape[0] // 2
        sent = value[half:].astype(jnp.bfloat16)
        value = value[:half].astype(jnp.float32) + swap(sent, mask).astype(jnp.float32)
    return value


NEAR_FAR = (CORE, NEAR, FAR)
FAR_NEAR = (CORE, FAR, NEAR)


def offset_of(place, order):
    total = jnp.zeros_like(place)
    for at, mask in enumerate(order):
        total = total + mask * ((place >> (2 - at)) & 1)
    return total


def place_of(offset, order):
    total = jnp.zeros_like(offset)
    for at, mask in enumerate(order):
        total = total + jnp.where((offset & mask) != 0, 1 << (2 - at), 0)
    return total


def picked(source, value):
    columns = lax.broadcasted_iota(jnp.int32, (source.shape[0], value.shape[0]), 1)
    chooser = (source[:, None] == columns).astype(jnp.bfloat16)
    return contract(chooser, value, 1, 0).astype(jnp.bfloat16)


def turned_contract(left, right):
    if left.shape[0] % 128 or right.shape[0] % 128:
        return contract(left, right, 1, 1)
    return contract(right, left, 1, 1).T


def estimate():
    return pl.CostEstimate(flops=1, bytes_accessed=1, transcendentals=0)


def params():
    return pltpu.CompilerParams(
        dimension_semantics=("arbitrary",), vmem_limit_bytes=44 * 1024 * 1024
    )


def tile_of(size, most):
    return most if size % most == 0 else size


def whole_block(part):
    return pl.BlockSpec(part.shape, lambda at: (0,) * part.ndim)


def run(kernel, operands, in_specs, out_specs, out_shape, grid, name, marks, aliases=None, scratch=()):
    count = len(operands)

    def body_of(*refs):
        kernel(*refs[:count], *refs[count + len(marks) :])

    return pl.pallas_call(
        body_of,
        grid=grid,
        in_specs=list(in_specs) + [pl.BlockSpec(memory_space=pl.ANY)] * len(marks),
        out_specs=out_specs,
        out_shape=out_shape,
        input_output_aliases=aliases or {},
        scratch_shapes=scratch,
        compiler_params=params(),
        cost_estimate=estimate(),
        name=name,
    )(*operands, *marks)


def hidden_parts(rows_in, rows_grad, up_block, down_block, first, width, *, marks):
    count, depth = rows_in.shape
    tile = tile_of(width, 512)
    skip = first // tile
    half = count // 2

    def kernel(in_ref, grad_ref, up_ref, down_ref, keep_ref, send_ref):
        pre = jnp.dot(in_ref[...], up_ref[...], preferred_element_type=jnp.float32)
        keep_ref[0] = pre[:half]
        send_ref[0] = pre[half:].astype(jnp.bfloat16)
        hidden = turned_contract(grad_ref[...], down_ref[...])
        keep_ref[1] = hidden[:half]
        send_ref[1] = hidden[half:].astype(jnp.bfloat16)

    return run(
        kernel,
        (rows_in, rows_grad, up_block, down_block),
        [
            whole_block(rows_in),
            whole_block(rows_grad),
            pl.BlockSpec((depth, tile), lambda at: (0, at + skip)),
            pl.BlockSpec((tile, depth), lambda at: (at + skip, 0)),
        ],
        [pl.BlockSpec((2, half, tile), lambda at: (0, 0, at))] * 2,
        (
            jax.ShapeDtypeStruct((2, half, width), jnp.float32),
            jax.ShapeDtypeStruct((2, half, width), jnp.bfloat16),
        ),
        (width // tile,),
        "hidden_parts",
        marks,
    )


def joined(pieces):
    if pieces[0].shape[0] % 16:
        return [jnp.concatenate(pieces, axis=0)]
    return pieces


def input_part(pieces, up_block, first, start=None, *, marks):
    pieces = joined(pieces)
    count = sum(piece.shape[0] for piece in pieces)
    depth = up_block.shape[0]
    width = pieces[0].shape[1]
    tile = tile_of(width, 512)
    skip = first // tile
    begin = [] if start is None else [start]

    last = width // tile - 1
    turned = count % 128 == 0

    def kernel(*refs):
        up_ref, out_ref = refs[len(pieces)], refs[-2]
        total_ref = refs[-1]
        rows = jnp.concatenate([ref[...] for ref in refs[: len(pieces)]], axis=0)
        part = contract(up_ref[...], rows, 1, 1) if turned else contract(rows, up_ref[...], 1, 1)

        @pl.when(pl.program_id(0) == 0)
        def _():
            total_ref[...] = part

        @pl.when(pl.program_id(0) != 0)
        def _():
            total_ref[...] += part

        @pl.when(pl.program_id(0) == last)
        def _():
            total = total_ref[...].T if turned else total_ref[...]
            out_ref[...] = total + refs[-3][...] if begin else total

    result = jax.ShapeDtypeStruct((count, depth), jnp.float32)
    return run(
        kernel,
        (*pieces, up_block, *begin),
        [pl.BlockSpec((piece.shape[0], tile), lambda at: (0, at)) for piece in pieces]
        + [pl.BlockSpec((depth, tile), lambda at: (0, at + skip))]
        + [whole_block(part) for part in begin],
        whole_block(result),
        result,
        (width // tile,),
        "input_part",
        marks,
        scratch=[pltpu.VMEM((depth, count) if turned else (count, depth), jnp.float32)],
    )


def up_gradient(turned, pieces, first, full, before=None, *, marks):
    pieces = joined(pieces)
    depth = turned.shape[0]
    width = pieces[0].shape[1]
    tile = tile_of(width, 512)
    skip = first // tile
    begin = [] if before is None else [before]

    def kernel(turned_ref, *refs):
        rows = jnp.concatenate([ref[...] for ref in refs[: len(pieces)]], axis=0)
        refs[-1][...] = jnp.zeros_like(refs[-1])
        refs[-2][...] = jnp.dot(
            turned_ref[...], rows, preferred_element_type=jnp.float32
        ).astype(jnp.bfloat16)

    mark = jax.ShapeDtypeStruct((8, 128), jnp.float32)
    return run(
        kernel,
        (turned, *pieces, *begin),
        [whole_block(turned)]
        + [pl.BlockSpec((piece.shape[0], tile), lambda at: (0, at)) for piece in pieces]
        + [pl.BlockSpec(memory_space=pl.ANY)] * len(begin),
        (pl.BlockSpec((depth, tile), lambda at: (0, at + skip)), whole_block(mark)),
        (jax.ShapeDtypeStruct((depth, full), jnp.bfloat16), mark),
        (width // tile,),
        "up_gradient",
        marks,
        {1 + len(pieces): 0} if begin else {},
    )


def down_gradient(pieces, rows_grad, first, full, before=None, *, marks):
    pieces = joined(pieces)
    depth = rows_grad.shape[1]
    width = pieces[0].shape[1]
    tile = tile_of(width, 512)
    skip = first // tile
    begin = [] if before is None else [before]

    def kernel(grad_ref, *refs):
        rows = jnp.concatenate([ref[...] for ref in refs[: len(pieces)]], axis=0)
        refs[-1][...] = jnp.zeros_like(refs[-1])
        refs[-2][...] = contract(rows, grad_ref[...], 0, 0).astype(jnp.bfloat16)

    mark = jax.ShapeDtypeStruct((8, 128), jnp.float32)
    return run(
        kernel,
        (rows_grad, *pieces, *begin),
        [whole_block(rows_grad)]
        + [pl.BlockSpec((piece.shape[0], tile), lambda at: (0, at)) for piece in pieces]
        + [pl.BlockSpec(memory_space=pl.ANY)] * len(begin),
        (pl.BlockSpec((tile, depth), lambda at: (at + skip, 0)), whole_block(mark)),
        (jax.ShapeDtypeStruct((full, depth), jnp.bfloat16), mark),
        (width // tile,),
        "down_gradient",
        marks,
        {1 + len(pieces): 0} if begin else {},
    )


def context_parts(rows_by_order, proj_block, *, marks):
    _, count, depth = rows_by_order.shape
    width = proj_block.shape[0]
    tile = tile_of(width // 2, 1024)
    each = width // 2 // tile
    half = count // 2

    def kernel(rows_ref, proj_ref, keep_ref, send_ref):
        part = turned_contract(rows_ref[0], proj_ref[...])
        keep_ref[...] = part[:half]
        send_ref[...] = part[half:].astype(jnp.bfloat16)

    return run(
        kernel,
        (rows_by_order, proj_block),
        [
            pl.BlockSpec((1, count, depth), lambda at: (at // each, 0, 0)),
            pl.BlockSpec((tile, depth), lambda at: (at, 0)),
        ],
        [pl.BlockSpec((half, tile), lambda at: (0, at))] * 2,
        (
            jax.ShapeDtypeStruct((half, width), jnp.float32),
            jax.ShapeDtypeStruct((half, width), jnp.bfloat16),
        ),
        (width // tile,),
        "context_parts",
        marks,
    )


def body(input_tiles, grad_tiles, context_tiles, up_tiles, down_tiles, output_tiles):
    grid_index = lax.axis_index("gx")
    total_bits = lax.axis_size("gx").bit_length() - 1
    q_masks = [1 << bit for bit in range(3, total_bits)]
    own_p = grid_index & (SHARES - 1)
    own_q = grid_index >> 3
    inputs = input_tiles[0]
    grads = grad_tiles[0]
    context = context_tiles[0]
    up_block = up_tiles[0]
    down_block = down_tiles[0]
    proj_block = output_tiles[0]
    rows = inputs.shape[0]
    half_rows = rows // 2
    share_rows = rows // SHARES
    block_rows = context.shape[0]
    half_block = block_rows // 2
    q_count = 1 << len(q_masks)
    width = up_block.shape[1]
    part_width = width // 2

    def row_source(order):
        at = jnp.arange(rows, dtype=jnp.int32)
        share = own_p ^ offset_of(at // share_rows, order)
        return share * share_rows + at % share_rows

    def half_source(half):
        at = jnp.arange(half_rows, dtype=jnp.int32)
        local = (at // GROUP) * 2 * GROUP + half * GROUP + at % GROUP
        place = place_of(own_p ^ (local // share_rows), NEAR_FAR)
        return place * share_rows + local % share_rows

    def token_source(half, order):
        at = jnp.arange(SHARES * half_block, dtype=jnp.int32)
        block = own_p ^ offset_of(at // half_block, order)
        at = at % half_block
        token = block * block_rows + (at // GROUP) * 2 * GROUP + half * GROUP + at % GROUP
        local = token % rows
        inside = (local // (2 * GROUP)) * GROUP + local % GROUP
        return ((token // rows) ^ own_q) * half_rows + inside

    def q_gather(value):
        value = value[None]
        for mask in q_masks:
            value = jnp.concatenate([value, swap(value, mask)], axis=0)
        return value

    source_nf = row_source(NEAR_FAR)
    own_rows = picked(source_nf, inputs), picked(row_source(FAR_NEAR), grads)
    pairs = [q_gather(part)[1:] for part in own_rows]
    groups = [
        [at + low for at in range(SHARES)] for low in range(0, lax.axis_size("gx"), SHARES)
    ]
    chunks = {"own": own_rows}
    grads_nf = picked(source_nf, grads)

    state, saved = {}, {}
    act_rows, dpre_rows = {}, {}
    late, alive = [own_rows[1]], []

    def corner(part):
        return part.reshape(-1, part.shape[-1])[:8, :128]

    def held(values):
        values, after = lax.optimization_barrier((values, corner(late[0])))
        alive.append(after)
        return values

    def marks():
        used = [*alive, corner(late[0])]
        alive.clear()
        return used

    def fetch(which):
        pairs[which] = held(pairs[which])
        late[0] = pairs[which]
        if which == 1:
            chunks["other"] = tuple(part.reshape((q_count - 1) * rows, -1) for part in pairs)

    def sums(name):
        chunk_in, chunk_grad = chunks[name[0]]
        keep, send = hidden_parts(
            chunk_in, chunk_grad, up_block, down_block, name[1] * part_width, part_width,
            marks=marks(),
        )
        state[name] = keep, swap(send, CORE)
        late[0] = send

    def summed(parts, which, at):
        keep, recv, *more = parts
        total = keep[which, at] + recv[which, at].astype(jnp.float32)
        for part in more:
            total = total + part[which][at].astype(jnp.float32)
        return total

    def halved(parts, which):
        count = parts[-1][which].shape[0] // 2
        return summed(parts, which, slice(count, 2 * count)).astype(jnp.bfloat16)

    def sums_core(name):
        parts = held(state[name])
        send = halved(parts, 0), halved(parts, 1)
        state[name] = *parts, (swap(send[0], NEAR), swap(send[1], FAR))
        late[0] = send[0]

    def sums_one(name):
        parts = held(state[name])
        send = halved(parts, 0), halved(parts, 1)
        state[name] = *parts, (swap(send[0], FAR), swap(send[1], NEAR))
        late[0] = send[0]

    def gelu(name):
        parts = held(state[name])
        at = slice(0, parts[-1][0].shape[0])
        act, gelu_back = jax.vjp(gelu_tanh, summed(parts, 0, at))
        dpre = gelu_back(summed(parts, 1, at))[0].astype(jnp.bfloat16)
        act = act.astype(jnp.bfloat16)
        state[name] = dpre, act
        late[0] = dpre

    def spread(name):
        dpre, act = held(state[name])
        state[name] = dpre, act, swap(dpre, FAR), swap(act, NEAR)

    def spread_one(name):
        dpre, act, dpre_recv, act_recv = held(state[name])
        dpre = jnp.concatenate([dpre, dpre_recv], axis=0)
        act = jnp.concatenate([act, act_recv], axis=0)
        state[name] = dpre, act, swap(dpre, NEAR), swap(act, FAR)
        late[0] = dpre

    def spread_two(name):
        dpre, act, dpre_recv, act_recv = held(state[name])
        dpre_rows[name] = [dpre, dpre_recv, swap(dpre, CORE), swap(dpre_recv, CORE)]
        act_rows[name] = act, act_recv
        late[0] = dpre_recv

    def act_core(name):
        act = jnp.concatenate(held(act_rows[name]), axis=0)
        act_rows[name] = [act, swap(act, CORE)]
        late[0] = act

    parts = {}

    def back(name):
        part = input_part(
            dpre_rows[name], up_block, name[1] * part_width, parts.get(name[0]), marks=marks()
        )
        parts[name[0]] = part
        late[0] = part

    def q_sums():
        if q_count == 2:
            sent = held(parts["other"]).astype(jnp.bfloat16)
            parts["recv"] = swap(sent, q_masks[0])
            late[0] = sent

    halves, d_context_halves = {}, {}

    def finish_rows():
        if q_count == 2:
            own, recv = held((parts["own"], parts["recv"]))
            share = own + recv.astype(jnp.float32)
        else:
            other = parts["other"].reshape(q_count - 1, rows, -1)
            share = scatter(
                jnp.concatenate([parts["own"][None], other], axis=0), q_masks[::-1]
            )[0]
        d_input = (grads_nf.astype(jnp.float32) + share).astype(jnp.bfloat16)
        saved["d_input"] = d_input
        source = jnp.concatenate([half_source(0), half_source(1)])
        ordered = picked(source, d_input)
        for half in range(2):
            halves[half] = q_gather(ordered[half * half_rows : (half + 1) * half_rows])
        late[0] = ordered

    def context_sums(half):
        gathered = held(halves[half]).reshape(q_count * half_rows, -1)
        by_order = [picked(token_source(half, order), gathered) for order in (NEAR_FAR, FAR_NEAR)]
        saved["d_input", half] = gathered
        keep, send = context_parts(jnp.stack(by_order), proj_block, marks=marks())
        halves[half] = keep, swap(send, CORE)
        late[0] = send

    def context_summed(parts, which, at):
        keep, recv, *more = parts
        columns = keep.shape[1] // 2
        here = slice(which * columns, (which + 1) * columns)
        total = keep[at, here] + recv[at, here].astype(jnp.float32)
        for part in more:
            total = total + part[which][at].astype(jnp.float32)
        return total

    def context_halved(parts, which, count):
        return context_summed(parts, which, slice(count, 2 * count)).astype(jnp.bfloat16)

    def context_core(half):
        parts = held(halves[half])
        count = parts[1].shape[0] // 2
        sent = context_halved(parts, 0, count), context_halved(parts, 1, count)
        halves[half] = *parts, (swap(sent[0], NEAR), swap(sent[1], FAR))
        late[0] = sent[0]

    def context_one(half):
        parts = held(halves[half])
        count = parts[1].shape[0] // 4
        sent = context_halved(parts, 0, count), context_halved(parts, 1, count)
        halves[half] = *parts, (swap(sent[0], FAR), swap(sent[1], NEAR))
        late[0] = sent[0]

    def context_two(half):
        parts = held(halves[half])
        at = slice(0, parts[1].shape[0] // 4)
        first, second = context_summed(parts, 0, at), context_summed(parts, 1, at)
        d_context_halves[half] = jnp.concatenate([first, second], axis=1).astype(jnp.bfloat16)
        late[0] = d_context_halves[half]

    mine_a, mine_b, other_a, other_b = ("own", 0), ("own", 1), ("other", 0), ("other", 1)
    sums(mine_a)
    sums_core(mine_a)
    sums(mine_b)
    sums_one(mine_a)
    fetch(0)
    gelu(mine_a)
    spread(mine_a)
    sums_core(mine_b)
    fetch(1)
    in_all = jnp.concatenate([chunks[name][0] for name in ("own", "other")], axis=0)
    turned = in_all.T
    grad_all = jnp.concatenate([chunks[name][1] for name in ("own", "other")], axis=0)
    sums(other_a)
    sums_one(mine_b)
    spread_one(mine_a)
    gelu(mine_b)
    sums_core(other_a)
    sums(other_b)
    spread_two(mine_a)
    sums_one(other_a)
    back(mine_a)
    gelu(other_a)
    spread(other_a)
    sums_core(other_b)
    spread_one(other_a)
    sums_one(other_b)
    gelu(other_b)
    spread(other_b)
    spread_two(other_a)
    spread_one(other_b)
    back(other_a)
    spread(mine_b)
    act_core(mine_a)
    spread_two(other_b)
    spread_one(mine_b)
    context_all = lax.all_gather(held(context), "gx", axis_index_groups=groups, tiled=True)
    back(other_b)
    q_sums()
    act_core(other_a)
    spread_two(mine_b)
    pieces = [piece for name in (mine_a, other_a) for piece in dpre_rows[name]]
    d_up, late[0] = up_gradient(turned, pieces, 0, width, marks=marks())
    pieces = [piece for name in (mine_a, other_a) for piece in act_rows[name]]
    d_down, late[0] = down_gradient(pieces, grad_all, 0, width, marks=marks())
    act_core(other_b)
    back(mine_b)
    finish_rows()
    act_core(mine_b)
    pieces = [piece for name in (mine_b, other_b) for piece in dpre_rows[name]]
    d_up, late[0] = up_gradient(turned, pieces, part_width, width, d_up, marks=marks())
    pieces = [piece for name in (mine_b, other_b) for piece in act_rows[name]]
    d_down, late[0] = down_gradient(pieces, grad_all, part_width, width, d_down, marks=marks())
    context_all = held(context_all)
    context_sums(0)
    context_sums(1)
    context_core(0)
    context_core(1)
    tokens = jnp.arange(q_count * rows, dtype=jnp.int32)
    local = tokens % rows
    source = ((tokens // rows) ^ own_q) * half_rows + (local // (2 * GROUP)) * GROUP
    source = source + local % GROUP + ((local // GROUP) % 2) * q_count * half_rows
    both = jnp.concatenate([saved["d_input", 0], saved["d_input", 1]], axis=0)
    d_input_all = picked(source, both)
    d_output, late[0] = down_gradient(
        [context_all], d_input_all, 0, context_all.shape[1], marks=marks()
    )
    context_one(0)
    context_one(1)
    context_two(0)
    context_two(1)

    columns = lax.broadcasted_iota(jnp.int32, (rows, rows), 1)
    chooser = (source_nf[:, None] == columns).astype(jnp.bfloat16)
    d_input = contract(chooser, saved["d_input"], 0, 0).astype(jnp.bfloat16)

    split = [
        d_context_halves[half].reshape(block_rows // (2 * GROUP), 1, GROUP, -1)
        for half in range(2)
    ]
    d_context = jnp.concatenate(split, axis=1).reshape(block_rows, -1)
    return (d_input[None], d_context[None], d_up[None], d_down[None], d_output[None])


def solution(mesh):
    return jax.shard_map(
        body,
        mesh=mesh,
        in_specs=(
            P("gx", "groups", None),
            P("gx", "groups", None),
            P("gx", "groups", None),
            P("gx", None, None),
            P("gx", None, None),
            P("gx", None, None),
        ),
        out_specs=(
            P("gx", "groups", None),
            P("gx", "groups", None),
            P("gx", "groups", None),
            P("gx", "groups", None),
            P("gx", "groups", None),
        ),
        check_vma=False,
    )
```

```python
import jax
import jax.numpy as jnp
from jax import lax
from jax.experimental import pallas as pl
from jax.experimental.pallas import tpu as pltpu
from jax.sharding import PartitionSpec as P

CORE, NEAR, FAR = 1, 2, 4
SHARES = 8
GROUP = 16


def swap(value, mask):
    count = lax.axis_size("gx")
    return lax.ppermute(value, "gx", [(at, at ^ mask) for at in range(count)])


def gelu_tanh(value):
    return jax.nn.gelu(value, approximate=True)


def contract(left, right, left_dim, right_dim):
    return lax.dot_general(
        left, right, (((left_dim,), (right_dim,)), ((), ())), preferred_element_type=jnp.float32
    )


def gather(value, masks):
    for mask in masks:
        value = jnp.concatenate([value, swap(value, mask)], axis=0)
    return value


def scatter(value, masks):
    for mask in masks:
        half = value.shape[0] // 2
        sent = value[half:].astype(jnp.bfloat16)
        value = value[:half].astype(jnp.float32) + swap(sent, mask).astype(jnp.float32)
    return value


NEAR_FAR = (CORE, NEAR, FAR)
FAR_NEAR = (CORE, FAR, NEAR)


def offset_of(place, order):
    total = jnp.zeros_like(place)
    for at, mask in enumerate(order):
        total = total + mask * ((place >> (2 - at)) & 1)
    return total


def place_of(offset, order):
    total = jnp.zeros_like(offset)
    for at, mask in enumerate(order):
        total = total + jnp.where((offset & mask) != 0, 1 << (2 - at), 0)
    return total


def picked(source, value):
    columns = lax.broadcasted_iota(jnp.int32, (source.shape[0], value.shape[0]), 1)
    chooser = (source[:, None] == columns).astype(jnp.bfloat16)
    return contract(chooser, value, 1, 0).astype(jnp.bfloat16)


def turned_contract(left, right):
    if left.shape[0] % 128 or right.shape[0] % 128:
        return contract(left, right, 1, 1)
    return contract(right, left, 1, 1).T


def estimate():
    return pl.CostEstimate(flops=1, bytes_accessed=1, transcendentals=0)


def params(mebibytes):
    return pltpu.CompilerParams(
        dimension_semantics=("arbitrary",), vmem_limit_bytes=mebibytes * 1024 * 1024
    )


def tile_of(size, most):
    return most if size % most == 0 else size


def whole_block(part):
    return pl.BlockSpec(part.shape, lambda at: (0,) * part.ndim)


def run(kernel, operands, in_specs, out_specs, out_shape, grid, name, marks, aliases=None, scratch=(), memory=36):
    count = len(operands)

    def body_of(*refs):
        kernel(*refs[:count], *refs[count + len(marks) :])

    return pl.pallas_call(
        body_of,
        grid=grid,
        in_specs=list(in_specs) + [pl.BlockSpec(memory_space=pl.ANY)] * len(marks),
        out_specs=out_specs,
        out_shape=out_shape,
        input_output_aliases=aliases or {},
        scratch_shapes=scratch,
        compiler_params=params(memory),
        cost_estimate=estimate(),
        name=name,
    )(*operands, *marks)


def hidden_parts(rows_in, rows_grad, up_block, down_block, first, width, *, marks):
    count, depth = rows_in.shape
    tile = tile_of(width, 2048)
    skip = first // tile
    half = count // 2

    def kernel(in_ref, grad_ref, up_ref, down_ref, keep_ref, send_ref):
        pre = jnp.dot(in_ref[...], up_ref[...], preferred_element_type=jnp.float32)
        keep_ref[0] = pre[:half]
        send_ref[0] = pre[half:].astype(jnp.bfloat16)
        hidden = turned_contract(grad_ref[...], down_ref[...])
        keep_ref[1] = hidden[:half]
        send_ref[1] = hidden[half:].astype(jnp.bfloat16)

    return run(
        kernel,
        (rows_in, rows_grad, up_block, down_block),
        [
            whole_block(rows_in),
            whole_block(rows_grad),
            pl.BlockSpec((depth, tile), lambda at: (0, at + skip)),
            pl.BlockSpec((tile, depth), lambda at: (at + skip, 0)),
        ],
        [pl.BlockSpec((2, half, tile), lambda at: (0, 0, at))] * 2,
        (
            jax.ShapeDtypeStruct((2, half, width), jnp.float32),
            jax.ShapeDtypeStruct((2, half, width), jnp.bfloat16),
        ),
        (width // tile,),
        "hidden_parts",
        marks,
    )


def joined(pieces):
    if pieces[0].shape[0] % 16:
        return [jnp.concatenate(pieces, axis=0)]
    return pieces


def input_part(pieces, up_block, first, start=None, *, marks):
    pieces = joined(pieces)
    count = sum(piece.shape[0] for piece in pieces)
    depth = up_block.shape[0]
    width = pieces[0].shape[1]
    tile = tile_of(width, 2048)
    skip = first // tile
    begin = [] if start is None else [start]

    last = width // tile - 1
    turned = count % 128 == 0

    def kernel(*refs):
        up_ref, out_ref = refs[len(pieces)], refs[-2]
        total_ref = refs[-1]
        rows = jnp.concatenate([ref[...] for ref in refs[: len(pieces)]], axis=0)
        part = contract(up_ref[...], rows, 1, 1) if turned else contract(rows, up_ref[...], 1, 1)

        @pl.when(pl.program_id(0) == 0)
        def _():
            total_ref[...] = part

        @pl.when(pl.program_id(0) != 0)
        def _():
            total_ref[...] += part

        @pl.when(pl.program_id(0) == last)
        def _():
            total = total_ref[...].T if turned else total_ref[...]
            out_ref[...] = total + refs[-3][...] if begin else total

    result = jax.ShapeDtypeStruct((count, depth), jnp.float32)
    return run(
        kernel,
        (*pieces, up_block, *begin),
        [pl.BlockSpec((piece.shape[0], tile), lambda at: (0, at)) for piece in pieces]
        + [pl.BlockSpec((depth, tile), lambda at: (0, at + skip))]
        + [whole_block(part) for part in begin],
        whole_block(result),
        result,
        (width // tile,),
        "input_part",
        marks,
        memory=36,
        scratch=[pltpu.VMEM((depth, count) if turned else (count, depth), jnp.float32)],
    )


def up_gradient(turned, pieces, first, full, before=None, *, marks):
    pieces = joined(pieces)
    depth = turned.shape[0]
    width = pieces[0].shape[1]
    tile = tile_of(width, 2048)
    skip = first // tile
    begin = [] if before is None else [before]

    def kernel(turned_ref, *refs):
        rows = jnp.concatenate([ref[...] for ref in refs[: len(pieces)]], axis=0)
        refs[-1][...] = jnp.zeros_like(refs[-1])
        refs[-2][...] = jnp.dot(
            turned_ref[...], rows, preferred_element_type=jnp.float32
        ).astype(jnp.bfloat16)

    mark = jax.ShapeDtypeStruct((8, 128), jnp.float32)
    return run(
        kernel,
        (turned, *pieces, *begin),
        [whole_block(turned)]
        + [pl.BlockSpec((piece.shape[0], tile), lambda at: (0, at)) for piece in pieces]
        + [pl.BlockSpec(memory_space=pl.ANY)] * len(begin),
        (pl.BlockSpec((depth, tile), lambda at: (0, at + skip)), whole_block(mark)),
        (jax.ShapeDtypeStruct((depth, full), jnp.bfloat16), mark),
        (width // tile,),
        "up_gradient",
        marks,
        {1 + len(pieces): 0} if begin else {},
        memory=36,
    )


def down_gradient(pieces, rows_grad, first, full, before=None, *, marks):
    pieces = joined(pieces)
    depth = rows_grad.shape[1]
    width = pieces[0].shape[1]
    tile = tile_of(width, 2048)
    skip = first // tile
    begin = [] if before is None else [before]

    def kernel(grad_ref, *refs):
        rows = jnp.concatenate([ref[...] for ref in refs[: len(pieces)]], axis=0)
        refs[-1][...] = jnp.zeros_like(refs[-1])
        refs[-2][...] = contract(rows, grad_ref[...], 0, 0).astype(jnp.bfloat16)

    mark = jax.ShapeDtypeStruct((8, 128), jnp.float32)
    return run(
        kernel,
        (rows_grad, *pieces, *begin),
        [whole_block(rows_grad)]
        + [pl.BlockSpec((piece.shape[0], tile), lambda at: (0, at)) for piece in pieces]
        + [pl.BlockSpec(memory_space=pl.ANY)] * len(begin),
        (pl.BlockSpec((tile, depth), lambda at: (at + skip, 0)), whole_block(mark)),
        (jax.ShapeDtypeStruct((full, depth), jnp.bfloat16), mark),
        (width // tile,),
        "down_gradient",
        marks,
        {1 + len(pieces): 0} if begin else {},
        memory=36,
    )


def context_parts(rows_by_order, proj_block, *, marks):
    _, count, depth = rows_by_order.shape
    width = proj_block.shape[0]
    tile = tile_of(width // 2, 2048)
    each = width // 2 // tile
    half = count // 2

    def kernel(rows_ref, proj_ref, keep_ref, send_ref):
        part = turned_contract(rows_ref[0], proj_ref[...])
        keep_ref[...] = part[:half]
        send_ref[...] = part[half:].astype(jnp.bfloat16)

    return run(
        kernel,
        (rows_by_order, proj_block),
        [
            pl.BlockSpec((1, count, depth), lambda at: (at // each, 0, 0)),
            pl.BlockSpec((tile, depth), lambda at: (at, 0)),
        ],
        [pl.BlockSpec((half, tile), lambda at: (0, at))] * 2,
        (
            jax.ShapeDtypeStruct((half, width), jnp.float32),
            jax.ShapeDtypeStruct((half, width), jnp.bfloat16),
        ),
        (width // tile,),
        "context_parts",
        marks,
    )


def body(input_tiles, grad_tiles, context_tiles, up_tiles, down_tiles, output_tiles):
    grid_index = lax.axis_index("gx")
    total_bits = lax.axis_size("gx").bit_length() - 1
    q_masks = [1 << bit for bit in range(3, total_bits)]
    own_p = grid_index & (SHARES - 1)
    own_q = grid_index >> 3
    inputs = input_tiles[0]
    grads = grad_tiles[0]
    context = context_tiles[0]
    up_block = up_tiles[0]
    down_block = down_tiles[0]
    proj_block = output_tiles[0]
    rows = inputs.shape[0]
    half_rows = rows // 2
    share_rows = rows // SHARES
    block_rows = context.shape[0]
    half_block = block_rows // 2
    q_count = 1 << len(q_masks)
    width = up_block.shape[1]
    part_width = width // 2

    def row_source(order):
        at = jnp.arange(rows, dtype=jnp.int32)
        share = own_p ^ offset_of(at // share_rows, order)
        return share * share_rows + at % share_rows

    def half_source(half):
        at = jnp.arange(half_rows, dtype=jnp.int32)
        local = (at // GROUP) * 2 * GROUP + half * GROUP + at % GROUP
        place = place_of(own_p ^ (local // share_rows), NEAR_FAR)
        return place * share_rows + local % share_rows

    def token_source(half, order):
        at = jnp.arange(SHARES * half_block, dtype=jnp.int32)
        block = own_p ^ offset_of(at // half_block, order)
        at = at % half_block
        token = block * block_rows + (at // GROUP) * 2 * GROUP + half * GROUP + at % GROUP
        local = token % rows
        inside = (local // (2 * GROUP)) * GROUP + local % GROUP
        return ((token // rows) ^ own_q) * half_rows + inside

    def q_gather(value):
        value = value[None]
        for mask in q_masks:
            value = jnp.concatenate([value, swap(value, mask)], axis=0)
        return value

    source_nf = row_source(NEAR_FAR)
    own_rows = picked(source_nf, inputs), picked(row_source(FAR_NEAR), grads)
    pairs = [q_gather(part)[1:] for part in own_rows]
    groups = [
        [at + low for at in range(SHARES)] for low in range(0, lax.axis_size("gx"), SHARES)
    ]
    chunks = {"own": own_rows}
    grads_nf = picked(source_nf, grads)

    state, saved = {}, {}
    act_rows, dpre_rows = {}, {}
    late, alive = [own_rows[1]], []

    def corner(part):
        return part.reshape(-1, part.shape[-1])[:8, :128]

    def held(values):
        values, after = lax.optimization_barrier((values, corner(late[0])))
        alive.append(after)
        return values

    def marks():
        used = [*alive, corner(late[0])]
        alive.clear()
        return used

    def fetch(which):
        pairs[which] = held(pairs[which])
        late[0] = pairs[which]
        if which == 1:
            chunks["other"] = tuple(part.reshape((q_count - 1) * rows, -1) for part in pairs)

    def sums(name):
        chunk_in, chunk_grad = chunks[name[0]]
        keep, send = hidden_parts(
            chunk_in, chunk_grad, up_block, down_block, name[1] * part_width, part_width,
            marks=marks(),
        )
        state[name] = keep, swap(send, CORE)
        late[0] = send

    def summed(parts, which, at):
        keep, recv, *more = parts
        total = keep[which, at] + recv[which, at].astype(jnp.float32)
        for part in more:
            total = total + part[which][at].astype(jnp.float32)
        return total

    def halved(parts, which):
        count = parts[-1][which].shape[0] // 2
        return summed(parts, which, slice(count, 2 * count)).astype(jnp.bfloat16)

    def sums_core(name):
        parts = held(state[name])
        send = halved(parts, 0), halved(parts, 1)
        state[name] = *parts, (swap(send[0], NEAR), swap(send[1], FAR))
        late[0] = send[0]

    def sums_one(name):
        parts = held(state[name])
        send = halved(parts, 0), halved(parts, 1)
        state[name] = *parts, (swap(send[0], FAR), swap(send[1], NEAR))
        late[0] = send[0]

    def gelu(name):
        parts = held(state[name])
        at = slice(0, parts[-1][0].shape[0])
        act, gelu_back = jax.vjp(gelu_tanh, summed(parts, 0, at))
        dpre = gelu_back(summed(parts, 1, at))[0].astype(jnp.bfloat16)
        act = act.astype(jnp.bfloat16)
        state[name] = dpre, act
        late[0] = dpre

    def spread(name):
        dpre, act = held(state[name])
        state[name] = dpre, act, swap(dpre, FAR), swap(act, NEAR)

    def spread_one(name):
        dpre, act, dpre_recv, act_recv = held(state[name])
        dpre, act = held((
            jnp.concatenate([dpre, dpre_recv], axis=0), jnp.concatenate([act, act_recv], axis=0)
        ))
        state[name] = dpre, act, swap(dpre, NEAR), swap(act, FAR)
        late[0] = dpre

    def spread_two(name):
        dpre, act, dpre_recv, act_recv = held(state[name])
        dpre_rows[name] = [dpre, dpre_recv, swap(dpre, CORE), swap(dpre_recv, CORE)]
        act_rows[name] = act, act_recv
        late[0] = dpre_recv

    def act_core(name):
        act = held(jnp.concatenate(held(act_rows[name]), axis=0))
        act_rows[name] = [act, swap(act, CORE)]
        late[0] = act

    parts = {}

    def back(name):
        part = input_part(
            dpre_rows[name], up_block, name[1] * part_width, parts.get(name[0]), marks=marks()
        )
        parts[name[0]] = part
        late[0] = part

    def q_sums():
        if q_count == 2:
            sent = held(parts["other"]).astype(jnp.bfloat16)
            parts["recv"] = swap(sent, q_masks[0])
            late[0] = sent

    halves, d_context_halves = {}, {}

    def finish_rows():
        if q_count == 2:
            own, recv = held((parts["own"], parts["recv"]))
            share = own + recv.astype(jnp.float32)
        else:
            other = parts["other"].reshape(q_count - 1, rows, -1)
            share = scatter(
                jnp.concatenate([parts["own"][None], other], axis=0), q_masks[::-1]
            )[0]
        d_input = (grads_nf.astype(jnp.float32) + share).astype(jnp.bfloat16)
        saved["d_input"] = d_input
        source = jnp.concatenate([half_source(0), half_source(1)])
        ordered = picked(source, d_input)
        for half in range(2):
            halves[half] = q_gather(ordered[half * half_rows : (half + 1) * half_rows])
        late[0] = ordered

    def context_sums(half):
        gathered = held(halves[half]).reshape(q_count * half_rows, -1)
        by_order = [picked(token_source(half, order), gathered) for order in (NEAR_FAR, FAR_NEAR)]
        saved["d_input", half] = gathered
        keep, send = context_parts(jnp.stack(by_order), proj_block, marks=marks())
        halves[half] = keep, swap(send, CORE)
        late[0] = send

    def context_summed(parts, which, at):
        keep, recv, *more = parts
        columns = keep.shape[1] // 2
        here = slice(which * columns, (which + 1) * columns)
        total = keep[at, here] + recv[at, here].astype(jnp.float32)
        for part in more:
            total = total + part[which][at].astype(jnp.float32)
        return total

    def context_halved(parts, which, count):
        return context_summed(parts, which, slice(count, 2 * count)).astype(jnp.bfloat16)

    def context_core(half):
        parts = held(halves[half])
        count = parts[1].shape[0] // 2
        sent = context_halved(parts, 0, count), context_halved(parts, 1, count)
        halves[half] = *parts, (swap(sent[0], NEAR), swap(sent[1], FAR))
        late[0] = sent[0]

    def context_one(half):
        parts = held(halves[half])
        count = parts[1].shape[0] // 4
        sent = context_halved(parts, 0, count), context_halved(parts, 1, count)
        halves[half] = *parts, (swap(sent[0], FAR), swap(sent[1], NEAR))
        late[0] = sent[0]

    def context_two(half):
        parts = held(halves[half])
        at = slice(0, parts[1].shape[0] // 4)
        first, second = context_summed(parts, 0, at), context_summed(parts, 1, at)
        d_context_halves[half] = jnp.concatenate([first, second], axis=1).astype(jnp.bfloat16)
        late[0] = d_context_halves[half]

    mine_a, mine_b, other_a, other_b = ("own", 0), ("own", 1), ("other", 0), ("other", 1)
    sums(mine_a)
    sums_core(mine_a)
    sums(mine_b)
    sums_one(mine_a)
    fetch(0)
    gelu(mine_a)
    spread(mine_a)
    sums_core(mine_b)
    fetch(1)
    in_all = jnp.concatenate([chunks[name][0] for name in ("own", "other")], axis=0)
    turned = in_all.T
    grad_all = jnp.concatenate([chunks[name][1] for name in ("own", "other")], axis=0)
    sums(other_a)
    sums_one(mine_b)
    spread_one(mine_a)
    gelu(mine_b)
    sums_core(other_a)
    sums(other_b)
    spread_two(mine_a)
    sums_one(other_a)
    back(mine_a)
    gelu(other_a)
    spread(other_a)
    sums_core(other_b)
    spread_one(other_a)
    sums_one(other_b)
    gelu(other_b)
    spread(other_b)
    spread_two(other_a)
    spread_one(other_b)
    back(other_a)
    spread(mine_b)
    act_core(mine_a)
    spread_two(other_b)
    spread_one(mine_b)
    context_all = lax.all_gather(held(context), "gx", axis_index_groups=groups, tiled=True)
    pieces = [piece for name in (mine_a, other_a) for piece in dpre_rows[name]]
    d_up, late[0] = up_gradient(turned, pieces, 0, width, marks=marks())
    back(other_b)
    q_sums()
    spread_two(mine_b)
    act_core(other_a)
    pieces = [piece for name in (mine_a, other_a) for piece in act_rows[name]]
    d_down, late[0] = down_gradient(pieces, grad_all, 0, width, marks=marks())
    act_core(other_b)
    act_core(mine_b)
    back(mine_b)
    finish_rows()
    pieces = [piece for name in (mine_b, other_b) for piece in dpre_rows[name]]
    d_up, late[0] = up_gradient(turned, pieces, part_width, width, d_up, marks=marks())
    pieces = [piece for name in (mine_b, other_b) for piece in act_rows[name]]
    d_down, late[0] = down_gradient(pieces, grad_all, part_width, width, d_down, marks=marks())
    context_all = held(context_all)
    context_sums(0)
    context_sums(1)
    context_core(0)
    context_core(1)
    tokens = jnp.arange(q_count * rows, dtype=jnp.int32)
    local = tokens % rows
    source = ((tokens // rows) ^ own_q) * half_rows + (local // (2 * GROUP)) * GROUP
    source = source + local % GROUP + ((local // GROUP) % 2) * q_count * half_rows
    both = jnp.concatenate([saved["d_input", 0], saved["d_input", 1]], axis=0)
    d_input_all = picked(source, both)
    d_output, late[0] = down_gradient(
        [context_all], d_input_all, 0, context_all.shape[1], marks=marks()
    )
    context_one(0)
    context_one(1)
    context_two(0)
    context_two(1)

    columns = lax.broadcasted_iota(jnp.int32, (rows, rows), 1)
    chooser = (source_nf[:, None] == columns).astype(jnp.bfloat16)
    d_input = contract(chooser, saved["d_input"], 0, 0).astype(jnp.bfloat16)

    split = [
        d_context_halves[half].reshape(block_rows // (2 * GROUP), 1, GROUP, -1)
        for half in range(2)
    ]
    d_context = jnp.concatenate(split, axis=1).reshape(block_rows, -1)
    return (d_input[None], d_context[None], d_up[None], d_down[None], d_output[None])


def solution(mesh):
    return jax.shard_map(
        body,
        mesh=mesh,
        in_specs=(
            P("gx", "groups", None),
            P("gx", "groups", None),
            P("gx", "groups", None),
            P("gx", None, None),
            P("gx", None, None),
            P("gx", None, None),
        ),
        out_specs=(
            P("gx", "groups", None),
            P("gx", "groups", None),
            P("gx", "groups", None),
            P("gx", "groups", None),
            P("gx", "groups", None),
        ),
        check_vma=False,
    )
```

```python
import jax
import jax.numpy as jnp
from jax import lax
from jax.experimental import pallas as pl
from jax.experimental.pallas import tpu as pltpu
from jax.sharding import PartitionSpec as P

CORE, NEAR, FAR = 1, 2, 4
SHARES = 8
GROUP = 16


def swap(value, mask):
    count = lax.axis_size("gx")
    return lax.ppermute(value, "gx", [(at, at ^ mask) for at in range(count)])


def gelu_tanh(value):
    return jax.nn.gelu(value, approximate=True)


def contract(left, right, left_dim, right_dim):
    return lax.dot_general(
        left, right, (((left_dim,), (right_dim,)), ((), ())), preferred_element_type=jnp.float32
    )


def gather(value, masks):
    for mask in masks:
        value = jnp.concatenate([value, swap(value, mask)], axis=0)
    return value


def scatter(value, masks):
    for mask in masks:
        half = value.shape[0] // 2
        sent = value[half:].astype(jnp.bfloat16)
        value = value[:half].astype(jnp.float32) + swap(sent, mask).astype(jnp.float32)
    return value


NEAR_FAR = (CORE, NEAR, FAR)
FAR_NEAR = (CORE, FAR, NEAR)


def offset_of(place, order):
    total = jnp.zeros_like(place)
    for at, mask in enumerate(order):
        total = total + mask * ((place >> (2 - at)) & 1)
    return total


def place_of(offset, order):
    total = jnp.zeros_like(offset)
    for at, mask in enumerate(order):
        total = total + jnp.where((offset & mask) != 0, 1 << (2 - at), 0)
    return total


def picked(source, value):
    columns = lax.broadcasted_iota(jnp.int32, (source.shape[0], value.shape[0]), 1)
    chooser = (source[:, None] == columns).astype(jnp.bfloat16)
    return contract(chooser, value, 1, 0).astype(jnp.bfloat16)


def turned_contract(left, right):
    if left.shape[0] % 128 or right.shape[0] % 128:
        return contract(left, right, 1, 1)
    return contract(right, left, 1, 1).T


def estimate():
    return pl.CostEstimate(flops=1, bytes_accessed=1, transcendentals=0)


def params(mebibytes):
    return pltpu.CompilerParams(
        dimension_semantics=("arbitrary",), vmem_limit_bytes=mebibytes * 1024 * 1024
    )


def tile_of(size, most):
    return most if size % most == 0 else size


def whole_block(part):
    return pl.BlockSpec(part.shape, lambda at: (0,) * part.ndim)


def run(kernel, operands, in_specs, out_specs, out_shape, grid, name, marks, aliases=None, scratch=(), memory=36):
    count = len(operands)

    def body_of(*refs):
        kernel(*refs[:count], *refs[count + len(marks) :])

    return pl.pallas_call(
        body_of,
        grid=grid,
        in_specs=list(in_specs) + [pl.BlockSpec(memory_space=pl.ANY)] * len(marks),
        out_specs=out_specs,
        out_shape=out_shape,
        input_output_aliases=aliases or {},
        scratch_shapes=scratch,
        compiler_params=params(memory),
        cost_estimate=estimate(),
        name=name,
    )(*operands, *marks)


def hidden_parts(rows_in, rows_grad, up_block, down_block, first, width, *, marks):
    count, depth = rows_in.shape
    tile = tile_of(width, 2048)
    skip = first // tile
    half = count // 2

    def kernel(in_ref, grad_ref, up_ref, down_ref, keep_ref, send_ref):
        pre = jnp.dot(in_ref[...], up_ref[...], preferred_element_type=jnp.float32)
        keep_ref[0] = pre[:half]
        send_ref[0] = pre[half:].astype(jnp.bfloat16)
        hidden = turned_contract(grad_ref[...], down_ref[...])
        keep_ref[1] = hidden[:half]
        send_ref[1] = hidden[half:].astype(jnp.bfloat16)

    return run(
        kernel,
        (rows_in, rows_grad, up_block, down_block),
        [
            whole_block(rows_in),
            whole_block(rows_grad),
            pl.BlockSpec((depth, tile), lambda at: (0, at + skip)),
            pl.BlockSpec((tile, depth), lambda at: (at + skip, 0)),
        ],
        [pl.BlockSpec((2, half, tile), lambda at: (0, 0, at))] * 2,
        (
            jax.ShapeDtypeStruct((2, half, width), jnp.float32),
            jax.ShapeDtypeStruct((2, half, width), jnp.bfloat16),
        ),
        (width // tile,),
        "hidden_parts",
        marks,
    )


def joined(pieces):
    if pieces[0].shape[0] % 16:
        return [jnp.concatenate(pieces, axis=0)]
    return pieces


def input_part(pieces, up_block, first, start=None, *, marks):
    pieces = joined(pieces)
    count = sum(piece.shape[0] for piece in pieces)
    depth = up_block.shape[0]
    width = pieces[0].shape[1]
    tile = tile_of(width, 2048)
    skip = first // tile
    begin = [] if start is None else [start]

    last = width // tile - 1
    turned = count % 128 == 0

    def kernel(*refs):
        up_ref, out_ref = refs[len(pieces)], refs[-2]
        total_ref = refs[-1]
        rows = jnp.concatenate([ref[...] for ref in refs[: len(pieces)]], axis=0)
        part = contract(up_ref[...], rows, 1, 1) if turned else contract(rows, up_ref[...], 1, 1)

        @pl.when(pl.program_id(0) == 0)
        def _():
            total_ref[...] = part

        @pl.when(pl.program_id(0) != 0)
        def _():
            total_ref[...] += part

        @pl.when(pl.program_id(0) == last)
        def _():
            total = total_ref[...].T if turned else total_ref[...]
            out_ref[...] = total + refs[-3][...] if begin else total

    result = jax.ShapeDtypeStruct((count, depth), jnp.float32)
    return run(
        kernel,
        (*pieces, up_block, *begin),
        [pl.BlockSpec((piece.shape[0], tile), lambda at: (0, at)) for piece in pieces]
        + [pl.BlockSpec((depth, tile), lambda at: (0, at + skip))]
        + [whole_block(part) for part in begin],
        whole_block(result),
        result,
        (width // tile,),
        "input_part",
        marks,
        memory=36,
        scratch=[pltpu.VMEM((depth, count) if turned else (count, depth), jnp.float32)],
    )


def up_gradient(turned, pieces, first, full, before=None, *, marks):
    pieces = joined(pieces)
    depth = turned.shape[0]
    width = pieces[0].shape[1]
    tile = tile_of(width, 2048)
    skip = first // tile
    begin = [] if before is None else [before]

    def kernel(turned_ref, *refs):
        rows = jnp.concatenate([ref[...] for ref in refs[: len(pieces)]], axis=0)
        refs[-1][...] = jnp.zeros_like(refs[-1])
        refs[-2][...] = jnp.dot(
            turned_ref[...], rows, preferred_element_type=jnp.float32
        ).astype(jnp.bfloat16)

    mark = jax.ShapeDtypeStruct((8, 128), jnp.float32)
    return run(
        kernel,
        (turned, *pieces, *begin),
        [whole_block(turned)]
        + [pl.BlockSpec((piece.shape[0], tile), lambda at: (0, at)) for piece in pieces]
        + [pl.BlockSpec(memory_space=pl.ANY)] * len(begin),
        (pl.BlockSpec((depth, tile), lambda at: (0, at + skip)), whole_block(mark)),
        (jax.ShapeDtypeStruct((depth, full), jnp.bfloat16), mark),
        (width // tile,),
        "up_gradient",
        marks,
        {1 + len(pieces): 0} if begin else {},
        memory=62,
    )


def down_gradient(pieces, rows_grad, first, full, before=None, *, marks):
    pieces = joined(pieces)
    depth = rows_grad.shape[1]
    width = pieces[0].shape[1]
    tile = tile_of(width, 2048)
    skip = first // tile
    begin = [] if before is None else [before]

    def kernel(grad_ref, *refs):
        rows = jnp.concatenate([ref[...] for ref in refs[: len(pieces)]], axis=0)
        refs[-1][...] = jnp.zeros_like(refs[-1])
        refs[-2][...] = contract(rows, grad_ref[...], 0, 0).astype(jnp.bfloat16)

    mark = jax.ShapeDtypeStruct((8, 128), jnp.float32)
    return run(
        kernel,
        (rows_grad, *pieces, *begin),
        [whole_block(rows_grad)]
        + [pl.BlockSpec((piece.shape[0], tile), lambda at: (0, at)) for piece in pieces]
        + [pl.BlockSpec(memory_space=pl.ANY)] * len(begin),
        (pl.BlockSpec((tile, depth), lambda at: (at + skip, 0)), whole_block(mark)),
        (jax.ShapeDtypeStruct((full, depth), jnp.bfloat16), mark),
        (width // tile,),
        "down_gradient",
        marks,
        {1 + len(pieces): 0} if begin else {},
        memory=62,
    )


def context_parts(rows_by_order, proj_block, *, marks):
    _, count, depth = rows_by_order.shape
    width = proj_block.shape[0]
    tile = tile_of(width // 2, 2048)
    each = width // 2 // tile
    half = count // 2

    def kernel(rows_ref, proj_ref, keep_ref, send_ref):
        part = turned_contract(rows_ref[0], proj_ref[...])
        keep_ref[...] = part[:half]
        send_ref[...] = part[half:].astype(jnp.bfloat16)

    return run(
        kernel,
        (rows_by_order, proj_block),
        [
            pl.BlockSpec((1, count, depth), lambda at: (at // each, 0, 0)),
            pl.BlockSpec((tile, depth), lambda at: (at, 0)),
        ],
        [pl.BlockSpec((half, tile), lambda at: (0, at))] * 2,
        (
            jax.ShapeDtypeStruct((half, width), jnp.float32),
            jax.ShapeDtypeStruct((half, width), jnp.bfloat16),
        ),
        (width // tile,),
        "context_parts",
        marks,
        memory=62,
    )


def body(input_tiles, grad_tiles, context_tiles, up_tiles, down_tiles, output_tiles):
    grid_index = lax.axis_index("gx")
    total_bits = lax.axis_size("gx").bit_length() - 1
    q_masks = [1 << bit for bit in range(3, total_bits)]
    own_p = grid_index & (SHARES - 1)
    own_q = grid_index >> 3
    inputs = input_tiles[0]
    grads = grad_tiles[0]
    context = context_tiles[0]
    up_block = up_tiles[0]
    down_block = down_tiles[0]
    proj_block = output_tiles[0]
    rows = inputs.shape[0]
    half_rows = rows // 2
    share_rows = rows // SHARES
    block_rows = context.shape[0]
    half_block = block_rows // 2
    q_count = 1 << len(q_masks)
    width = up_block.shape[1]
    part_width = width // 2

    def row_source(order):
        at = jnp.arange(rows, dtype=jnp.int32)
        share = own_p ^ offset_of(at // share_rows, order)
        return share * share_rows + at % share_rows

    def half_source(half):
        at = jnp.arange(half_rows, dtype=jnp.int32)
        local = (at // GROUP) * 2 * GROUP + half * GROUP + at % GROUP
        place = place_of(own_p ^ (local // share_rows), NEAR_FAR)
        return place * share_rows + local % share_rows

    def token_source(half, order):
        at = jnp.arange(SHARES * half_block, dtype=jnp.int32)
        block = own_p ^ offset_of(at // half_block, order)
        at = at % half_block
        token = block * block_rows + (at // GROUP) * 2 * GROUP + half * GROUP + at % GROUP
        local = token % rows
        inside = (local // (2 * GROUP)) * GROUP + local % GROUP
        return ((token // rows) ^ own_q) * half_rows + inside

    def q_gather(value):
        value = value[None]
        for mask in q_masks:
            value = jnp.concatenate([value, swap(value, mask)], axis=0)
        return value

    def q_pieces(value):
        pieces = [value]
        for mask in q_masks:
            pieces = pieces + [swap(jnp.concatenate(pieces, axis=0), mask)]
        return pieces

    source_nf = row_source(NEAR_FAR)
    own_rows = picked(source_nf, inputs), picked(row_source(FAR_NEAR), grads)
    pairs = [q_gather(part)[1:] for part in own_rows]
    groups = [
        [at + low for at in range(SHARES)] for low in range(0, lax.axis_size("gx"), SHARES)
    ]
    chunks = {"own": own_rows}
    grads_nf = picked(source_nf, grads)

    state, saved = {}, {}
    act_rows, dpre_rows = {}, {}
    late, alive = [own_rows[1]], []

    def corner(part):
        return part.reshape(-1, part.shape[-1])[:8, :128]

    def held(values):
        values, after = lax.optimization_barrier((values, corner(late[0])))
        alive.append(after)
        return values

    def marks():
        used = [*alive, corner(late[0])]
        alive.clear()
        return used

    def fetch(which):
        pairs[which] = held(pairs[which])
        late[0] = pairs[which]
        if which == 1:
            chunks["other"] = tuple(part.reshape((q_count - 1) * rows, -1) for part in pairs)

    def sums(name):
        chunk_in, chunk_grad = chunks[name[0]]
        keep, send = hidden_parts(
            chunk_in, chunk_grad, up_block, down_block, name[1] * part_width, part_width,
            marks=marks(),
        )
        state[name] = keep, swap(send, CORE)
        late[0] = send

    def summed(parts, which, at):
        keep, recv, *more = parts
        total = keep[which, at] + recv[which, at].astype(jnp.float32)
        for part in more:
            total = total + part[which][at].astype(jnp.float32)
        return total

    def halved(parts, which):
        count = parts[-1][which].shape[0] // 2
        return summed(parts, which, slice(count, 2 * count)).astype(jnp.bfloat16)

    def sums_core(name):
        parts = held(state[name])
        send = halved(parts, 0), halved(parts, 1)
        state[name] = *parts, (swap(send[0], NEAR), swap(send[1], FAR))
        late[0] = send[0]

    def sums_one(name):
        parts = held(state[name])
        send = halved(parts, 0), halved(parts, 1)
        state[name] = *parts, (swap(send[0], FAR), swap(send[1], NEAR))
        late[0] = send[0]

    def gelu(name):
        parts = held(state[name])
        at = slice(0, parts[-1][0].shape[0])
        act, gelu_back = jax.vjp(gelu_tanh, summed(parts, 0, at))
        dpre = gelu_back(summed(parts, 1, at))[0].astype(jnp.bfloat16)
        act = act.astype(jnp.bfloat16)
        state[name] = dpre, act
        late[0] = dpre

    def spread(name):
        dpre, act = held(state[name])
        state[name] = dpre, act, swap(dpre, FAR), swap(act, NEAR)

    def spread_one(name):
        dpre, act, dpre_recv, act_recv = held(state[name])
        dpre, act = held((
            jnp.concatenate([dpre, dpre_recv], axis=0), jnp.concatenate([act, act_recv], axis=0)
        ))
        state[name] = dpre, act, swap(dpre, NEAR), swap(act, FAR)
        late[0] = dpre

    def spread_two(name):
        dpre, act, dpre_recv, act_recv = held(state[name])
        dpre_rows[name] = [dpre, dpre_recv, swap(dpre, CORE), swap(dpre_recv, CORE)]
        act_rows[name] = act, act_recv
        late[0] = dpre_recv

    def act_core(name):
        act = held(jnp.concatenate(held(act_rows[name]), axis=0))
        act_rows[name] = [act, swap(act, CORE)]
        late[0] = act

    parts = {}

    def back(name):
        part = input_part(
            dpre_rows[name], up_block, name[1] * part_width, parts.get(name[0]), marks=marks()
        )
        parts[name[0]] = part
        late[0] = part

    def q_sums():
        if q_count == 2:
            sent = held(parts["other"]).astype(jnp.bfloat16)
            parts["recv"] = swap(sent, q_masks[0])
            late[0] = sent

    halves, d_context_halves = {}, {}

    def finish_rows():
        if q_count == 2:
            own, recv = held((parts["own"], parts["recv"]))
            share = own + recv.astype(jnp.float32)
        else:
            other = parts["other"].reshape(q_count - 1, rows, -1)
            share = scatter(
                jnp.concatenate([parts["own"][None], other], axis=0), q_masks[::-1]
            )[0]
        d_input = (grads_nf.astype(jnp.float32) + share).astype(jnp.bfloat16)
        saved["d_input"] = d_input
        source = jnp.concatenate([half_source(0), half_source(1)])
        ordered = picked(source, d_input)
        halves[0] = q_pieces(ordered[:half_rows])
        saved["rest"] = ordered[half_rows:]
        late[0] = ordered

    def second_rows():
        halves[0], rest = held((halves[0], saved["rest"]))
        halves[1] = q_pieces(rest)
        late[0] = rest

    def context_sums(half):
        gathered = jnp.concatenate(held(halves[half]), axis=0)
        by_order = [picked(token_source(half, order), gathered) for order in (NEAR_FAR, FAR_NEAR)]
        saved["d_input", half] = gathered
        keep, send = context_parts(jnp.stack(by_order), proj_block, marks=marks())
        halves[half] = keep, swap(send, CORE)
        late[0] = send

    def context_summed(parts, which, at):
        keep, recv, *more = parts
        columns = keep.shape[1] // 2
        here = slice(which * columns, (which + 1) * columns)
        total = keep[at, here] + recv[at, here].astype(jnp.float32)
        for part in more:
            total = total + part[which][at].astype(jnp.float32)
        return total

    def context_halved(parts, which, count):
        return context_summed(parts, which, slice(count, 2 * count)).astype(jnp.bfloat16)

    def context_core(half):
        parts = held(halves[half])
        count = parts[1].shape[0] // 2
        sent = context_halved(parts, 0, count), context_halved(parts, 1, count)
        halves[half] = *parts, (swap(sent[0], NEAR), swap(sent[1], FAR))
        late[0] = sent[0]

    def context_one(half):
        parts = held(halves[half])
        count = parts[1].shape[0] // 4
        sent = context_halved(parts, 0, count), context_halved(parts, 1, count)
        halves[half] = *parts, (swap(sent[0], FAR), swap(sent[1], NEAR))
        late[0] = sent[0]

    def context_two(half):
        parts = held(halves[half])
        at = slice(0, parts[1].shape[0] // 4)
        first, second = context_summed(parts, 0, at), context_summed(parts, 1, at)
        d_context_halves[half] = jnp.concatenate([first, second], axis=1).astype(jnp.bfloat16)
        late[0] = d_context_halves[half]

    mine_a, mine_b, other_a, other_b = ("own", 0), ("own", 1), ("other", 0), ("other", 1)
    sums(mine_a)
    sums_core(mine_a)
    sums(mine_b)
    sums_one(mine_a)
    fetch(0)
    gelu(mine_a)
    spread(mine_a)
    sums_core(mine_b)
    fetch(1)
    in_all = jnp.concatenate([chunks[name][0] for name in ("own", "other")], axis=0)
    turned = in_all.T
    grad_all = jnp.concatenate([chunks[name][1] for name in ("own", "other")], axis=0)
    sums(other_a)
    sums_one(mine_b)
    spread_one(mine_a)
    gelu(mine_b)
    sums_core(other_a)
    sums(other_b)
    spread_two(mine_a)
    sums_one(other_a)
    back(mine_a)
    gelu(other_a)
    spread(other_a)
    sums_core(other_b)
    spread_one(other_a)
    sums_one(other_b)
    gelu(other_b)
    spread(other_b)
    spread_two(other_a)
    spread_one(other_b)
    back(other_a)
    spread(mine_b)
    act_core(mine_a)
    spread_two(other_b)
    spread_one(mine_b)
    context_all = lax.all_gather(held(context), "gx", axis_index_groups=groups, tiled=True)
    pieces = [piece for name in (mine_a, other_a) for piece in dpre_rows[name]]
    d_up, late[0] = up_gradient(turned, pieces, 0, width, marks=marks())
    back(other_b)
    q_sums()
    spread_two(mine_b)
    act_core(other_a)
    pieces = [piece for name in (mine_a, other_a) for piece in act_rows[name]]
    d_down, late[0] = down_gradient(pieces, grad_all, 0, width, marks=marks())
    act_core(other_b)
    act_core(mine_b)
    back(mine_b)
    finish_rows()
    pieces = [piece for name in (mine_b, other_b) for piece in dpre_rows[name]]
    d_up, late[0] = up_gradient(turned, pieces, part_width, width, d_up, marks=marks())
    second_rows()
    context_sums(0)
    context_core(0)
    pieces = [piece for name in (mine_b, other_b) for piece in act_rows[name]]
    d_down, late[0] = down_gradient(pieces, grad_all, part_width, width, d_down, marks=marks())
    context_all = held(context_all)
    context_sums(1)
    context_core(1)
    tokens = jnp.arange(q_count * rows, dtype=jnp.int32)
    local = tokens % rows
    source = ((tokens // rows) ^ own_q) * half_rows + (local // (2 * GROUP)) * GROUP
    source = source + local % GROUP + ((local // GROUP) % 2) * q_count * half_rows
    both = jnp.concatenate([saved["d_input", 0], saved["d_input", 1]], axis=0)
    d_input_all = picked(source, both)
    d_output, late[0] = down_gradient(
        [context_all], d_input_all, 0, context_all.shape[1], marks=marks()
    )
    context_one(0)
    context_one(1)
    context_two(0)
    context_two(1)

    columns = lax.broadcasted_iota(jnp.int32, (rows, rows), 1)
    chooser = (source_nf[:, None] == columns).astype(jnp.bfloat16)
    d_input = contract(chooser, saved["d_input"], 0, 0).astype(jnp.bfloat16)

    split = [
        d_context_halves[half].reshape(block_rows // (2 * GROUP), 1, GROUP, -1)
        for half in range(2)
    ]
    d_context = jnp.concatenate(split, axis=1).reshape(block_rows, -1)
    return (d_input[None], d_context[None], d_up[None], d_down[None], d_output[None])


def solution(mesh):
    return jax.shard_map(
        body,
        mesh=mesh,
        in_specs=(
            P("gx", "groups", None),
            P("gx", "groups", None),
            P("gx", "groups", None),
            P("gx", None, None),
            P("gx", None, None),
            P("gx", None, None),
        ),
        out_specs=(
            P("gx", "groups", None),
            P("gx", "groups", None),
            P("gx", "groups", None),
            P("gx", "groups", None),
            P("gx", "groups", None),
        ),
        check_vma=False,
    )
```

```python
import jax
import jax.numpy as jnp
from jax import lax
from jax.experimental import pallas as pl
from jax.experimental.pallas import tpu as pltpu
from jax.sharding import PartitionSpec as P

CORE, NEAR, FAR = 1, 2, 4
SHARES = 8


def swap(value, mask):
    count = lax.axis_size("gx")
    return lax.ppermute(value, "gx", [(at, at ^ mask) for at in range(count)])


def gelu_tanh(value):
    return jax.nn.gelu(value, approximate=True)


def contract(left, right, left_dim, right_dim):
    return lax.dot_general(
        left, right, (((left_dim,), (right_dim,)), ((), ())), preferred_element_type=jnp.float32
    )


def gather(value, masks):
    for mask in masks:
        value = jnp.concatenate([value, swap(value, mask)], axis=0)
    return value


def scatter(value, masks):
    for mask in masks:
        half = value.shape[0] // 2
        sent = value[half:].astype(jnp.bfloat16)
        value = value[:half].astype(jnp.float32) + swap(sent, mask).astype(jnp.float32)
    return value


NEAR_FAR = (CORE, NEAR, FAR)
FAR_NEAR = (CORE, FAR, NEAR)


def offset_of(place, order):
    total = jnp.zeros_like(place)
    for at, mask in enumerate(order):
        total = total + mask * ((place >> (2 - at)) & 1)
    return total


def place_of(offset, order):
    total = jnp.zeros_like(offset)
    for at, mask in enumerate(order):
        total = total + jnp.where((offset & mask) != 0, 1 << (2 - at), 0)
    return total


def picked(source, value):
    columns = lax.broadcasted_iota(jnp.int32, (source.shape[0], value.shape[0]), 1)
    chooser = (source[:, None] == columns).astype(jnp.bfloat16)
    return contract(chooser, value, 1, 0).astype(jnp.bfloat16)


def turned_contract(left, right):
    if left.shape[0] % 128 or right.shape[0] % 128:
        return contract(left, right, 1, 1)
    return contract(right, left, 1, 1).T


def estimate():
    return pl.CostEstimate(flops=1, bytes_accessed=1, transcendentals=0)


def params(mebibytes):
    return pltpu.CompilerParams(
        dimension_semantics=("arbitrary",), vmem_limit_bytes=mebibytes * 1024 * 1024
    )


def tile_of(size, most):
    return most if size % most == 0 else size


def whole_block(part):
    return pl.BlockSpec(part.shape, lambda at: (0,) * part.ndim)


def run(kernel, operands, in_specs, out_specs, out_shape, grid, name, marks, aliases=None, scratch=(), memory=36):
    count = len(operands)

    def body_of(*refs):
        kernel(*refs[:count], *refs[count + len(marks) :])

    return pl.pallas_call(
        body_of,
        grid=grid,
        in_specs=list(in_specs) + [pl.BlockSpec(memory_space=pl.ANY)] * len(marks),
        out_specs=out_specs,
        out_shape=out_shape,
        input_output_aliases=aliases or {},
        scratch_shapes=scratch,
        compiler_params=params(memory),
        cost_estimate=estimate(),
        name=name,
    )(*operands, *marks)


def hidden_parts(rows_in, rows_grad, up_block, down_block, first, width, *, marks):
    count, depth = rows_in.shape
    tile = tile_of(width, 2048)
    skip = first // tile
    half = count // 2

    def kernel(in_ref, grad_ref, up_ref, down_ref, keep_ref, send_ref):
        pre = jnp.dot(in_ref[...], up_ref[...], preferred_element_type=jnp.float32)
        keep_ref[0] = pre[:half]
        send_ref[0] = pre[half:].astype(jnp.bfloat16)
        hidden = turned_contract(grad_ref[...], down_ref[...])
        keep_ref[1] = hidden[:half]
        send_ref[1] = hidden[half:].astype(jnp.bfloat16)

    return run(
        kernel,
        (rows_in, rows_grad, up_block, down_block),
        [
            whole_block(rows_in),
            whole_block(rows_grad),
            pl.BlockSpec((depth, tile), lambda at: (0, at + skip)),
            pl.BlockSpec((tile, depth), lambda at: (at + skip, 0)),
        ],
        [pl.BlockSpec((2, half, tile), lambda at: (0, 0, at))] * 2,
        (
            jax.ShapeDtypeStruct((2, half, width), jnp.float32),
            jax.ShapeDtypeStruct((2, half, width), jnp.bfloat16),
        ),
        (width // tile,),
        "hidden_parts",
        marks,
    )


def joined(pieces):
    if pieces[0].shape[0] % 16:
        return [jnp.concatenate(pieces, axis=0)]
    return pieces


def input_part(pieces, up_block, first, start=None, *, marks):
    pieces = joined(pieces)
    count = sum(piece.shape[0] for piece in pieces)
    depth = up_block.shape[0]
    width = pieces[0].shape[1]
    tile = tile_of(width, 2048)
    skip = first // tile
    begin = [] if start is None else [start]

    last = width // tile - 1
    turned = count % 128 == 0

    def kernel(*refs):
        up_ref, out_ref = refs[len(pieces)], refs[-2]
        total_ref = refs[-1]
        rows = jnp.concatenate([ref[...] for ref in refs[: len(pieces)]], axis=0)
        part = contract(up_ref[...], rows, 1, 1) if turned else contract(rows, up_ref[...], 1, 1)

        @pl.when(pl.program_id(0) == 0)
        def _():
            total_ref[...] = part

        @pl.when(pl.program_id(0) != 0)
        def _():
            total_ref[...] += part

        @pl.when(pl.program_id(0) == last)
        def _():
            total = total_ref[...].T if turned else total_ref[...]
            out_ref[...] = total + refs[-3][...] if begin else total

    result = jax.ShapeDtypeStruct((count, depth), jnp.float32)
    return run(
        kernel,
        (*pieces, up_block, *begin),
        [pl.BlockSpec((piece.shape[0], tile), lambda at: (0, at)) for piece in pieces]
        + [pl.BlockSpec((depth, tile), lambda at: (0, at + skip))]
        + [whole_block(part) for part in begin],
        whole_block(result),
        result,
        (width // tile,),
        "input_part",
        marks,
        memory=36,
        scratch=[pltpu.VMEM((depth, count) if turned else (count, depth), jnp.float32)],
    )


def up_gradient(turned, pieces, first, full, before=None, *, marks):
    pieces = joined(pieces)
    depth = turned.shape[0]
    width = pieces[0].shape[1]
    tile = tile_of(width, 2048)
    skip = first // tile
    begin = [] if before is None else [before]

    def kernel(turned_ref, *refs):
        rows = jnp.concatenate([ref[...] for ref in refs[: len(pieces)]], axis=0)
        refs[-1][...] = jnp.zeros_like(refs[-1])
        refs[-2][...] = jnp.dot(
            turned_ref[...], rows, preferred_element_type=jnp.float32
        ).astype(jnp.bfloat16)

    mark = jax.ShapeDtypeStruct((8, 128), jnp.float32)
    return run(
        kernel,
        (turned, *pieces, *begin),
        [whole_block(turned)]
        + [pl.BlockSpec((piece.shape[0], tile), lambda at: (0, at)) for piece in pieces]
        + [pl.BlockSpec(memory_space=pl.ANY)] * len(begin),
        (pl.BlockSpec((depth, tile), lambda at: (0, at + skip)), whole_block(mark)),
        (jax.ShapeDtypeStruct((depth, full), jnp.bfloat16), mark),
        (width // tile,),
        "up_gradient",
        marks,
        {1 + len(pieces): 0} if begin else {},
        memory=62,
    )


def down_gradient(pieces, rows_grad, first, full, before=None, *, marks):
    pieces = joined(pieces)
    depth = rows_grad.shape[1]
    width = pieces[0].shape[1]
    tile = tile_of(width, 2048)
    skip = first // tile
    begin = [] if before is None else [before]

    def kernel(grad_ref, *refs):
        rows = jnp.concatenate([ref[...] for ref in refs[: len(pieces)]], axis=0)
        refs[-1][...] = jnp.zeros_like(refs[-1])
        refs[-2][...] = contract(rows, grad_ref[...], 0, 0).astype(jnp.bfloat16)

    mark = jax.ShapeDtypeStruct((8, 128), jnp.float32)
    return run(
        kernel,
        (rows_grad, *pieces, *begin),
        [whole_block(rows_grad)]
        + [pl.BlockSpec((piece.shape[0], tile), lambda at: (0, at)) for piece in pieces]
        + [pl.BlockSpec(memory_space=pl.ANY)] * len(begin),
        (pl.BlockSpec((tile, depth), lambda at: (at + skip, 0)), whole_block(mark)),
        (jax.ShapeDtypeStruct((full, depth), jnp.bfloat16), mark),
        (width // tile,),
        "down_gradient",
        marks,
        {1 + len(pieces): 0} if begin else {},
        memory=36,
    )


def context_parts(rows_by_order, proj_block, *, marks):
    _, count, depth = rows_by_order.shape
    width = proj_block.shape[0]
    tile = tile_of(width // 2, 2048)
    each = width // 2 // tile
    half = count // 2

    def kernel(rows_ref, proj_ref, keep_ref, send_ref):
        part = turned_contract(rows_ref[0], proj_ref[...])
        keep_ref[...] = part[:half]
        send_ref[...] = part[half:].astype(jnp.bfloat16)

    return run(
        kernel,
        (rows_by_order, proj_block),
        [
            pl.BlockSpec((1, count, depth), lambda at: (at // each, 0, 0)),
            pl.BlockSpec((tile, depth), lambda at: (at, 0)),
        ],
        [pl.BlockSpec((half, tile), lambda at: (0, at))] * 2,
        (
            jax.ShapeDtypeStruct((half, width), jnp.float32),
            jax.ShapeDtypeStruct((half, width), jnp.bfloat16),
        ),
        (width // tile,),
        "context_parts",
        marks,
    )


def side_by_side(first, second, *, marks):
    count, width = first.shape

    def kernel(first_ref, second_ref, out_ref):
        out_ref[:, :width] = first_ref[...]
        out_ref[:, width:] = second_ref[...]

    result = jax.ShapeDtypeStruct((count, 2 * width), first.dtype)
    return run(
        kernel,
        (first, second),
        [whole_block(first), whole_block(second)],
        whole_block(result),
        result,
        (1,),
        "side_by_side",
        marks,
    )


def body(input_tiles, grad_tiles, context_tiles, up_tiles, down_tiles, output_tiles):
    grid_index = lax.axis_index("gx")
    total_bits = lax.axis_size("gx").bit_length() - 1
    q_masks = [1 << bit for bit in range(3, total_bits)]
    own_p = grid_index & (SHARES - 1)
    own_q = grid_index >> 3
    inputs = input_tiles[0]
    grads = grad_tiles[0]
    context = context_tiles[0]
    up_block = up_tiles[0]
    down_block = down_tiles[0]
    proj_block = output_tiles[0]
    rows = inputs.shape[0]
    share_rows = rows // SHARES
    block_rows = context.shape[0]
    q_count = 1 << len(q_masks)
    width = up_block.shape[1]
    part_width = width // 2

    def row_source(order):
        at = jnp.arange(rows, dtype=jnp.int32)
        share = own_p ^ offset_of(at // share_rows, order)
        return share * share_rows + at % share_rows

    def row_of(token):
        local = token % rows
        place = place_of(own_p ^ (local // share_rows), NEAR_FAR)
        return ((token // rows) ^ own_q) * rows + place * share_rows + local % share_rows

    def token_source(order):
        at = jnp.arange(SHARES * block_rows, dtype=jnp.int32)
        block = own_p ^ offset_of(at // block_rows, order)
        return row_of(block * block_rows + at % block_rows)

    def q_pieces(value):
        pieces = [value]
        for mask in q_masks:
            pieces = pieces + [swap(jnp.concatenate(pieces, axis=0), mask)]
        return pieces

    def q_gather(value):
        value = value[None]
        for mask in q_masks:
            value = jnp.concatenate([value, swap(value, mask)], axis=0)
        return value

    source_nf = row_source(NEAR_FAR)
    own_rows = picked(source_nf, inputs), picked(row_source(FAR_NEAR), grads)
    pairs = [q_gather(part)[1:] for part in own_rows]
    groups = [
        [at + low for at in range(SHARES)] for low in range(0, lax.axis_size("gx"), SHARES)
    ]
    chunks = {"own": own_rows}
    grads_nf = picked(source_nf, grads)

    state, saved = {}, {}
    act_rows, dpre_rows = {}, {}
    late, alive = [own_rows[1]], []

    def corner(part):
        return part.reshape(-1, part.shape[-1])[:8, :128]

    def held(values):
        values, after = lax.optimization_barrier((values, corner(late[0])))
        alive.append(after)
        return values

    def marks():
        used = [*alive, corner(late[0])]
        alive.clear()
        return used

    def fetch(which):
        pairs[which] = held(pairs[which])
        late[0] = pairs[which]
        if which == 1:
            chunks["other"] = tuple(part.reshape((q_count - 1) * rows, -1) for part in pairs)

    def sums(name):
        chunk_in, chunk_grad = chunks[name[0]]
        keep, send = hidden_parts(
            chunk_in, chunk_grad, up_block, down_block, name[1] * part_width, part_width,
            marks=marks(),
        )
        state[name] = keep, swap(send, CORE)
        late[0] = send

    def summed(parts, which, at):
        keep, recv, *more = parts
        total = keep[which, at] + recv[which, at].astype(jnp.float32)
        for part in more:
            total = total + part[which][at].astype(jnp.float32)
        return total

    def halved(parts, which):
        count = parts[-1][which].shape[0] // 2
        return summed(parts, which, slice(count, 2 * count)).astype(jnp.bfloat16)

    def sums_core(name):
        parts = held(state[name])
        send = halved(parts, 0), halved(parts, 1)
        state[name] = *parts, (swap(send[0], NEAR), swap(send[1], FAR))
        late[0] = send[0]

    def sums_one(name):
        parts = held(state[name])
        send = halved(parts, 0), halved(parts, 1)
        state[name] = *parts, (swap(send[0], FAR), swap(send[1], NEAR))
        late[0] = send[0]

    def gelu(name):
        parts = held(state[name])
        at = slice(0, parts[-1][0].shape[0])
        act, gelu_back = jax.vjp(gelu_tanh, summed(parts, 0, at))
        dpre = gelu_back(summed(parts, 1, at))[0].astype(jnp.bfloat16)
        act = act.astype(jnp.bfloat16)
        state[name] = dpre, act
        late[0] = dpre

    def spread(name):
        dpre, act = held(state[name])
        state[name] = dpre, act, swap(dpre, FAR), swap(act, NEAR)

    def spread_one(name):
        dpre, act, dpre_recv, act_recv = held(state[name])
        dpre, act = held((
            jnp.concatenate([dpre, dpre_recv], axis=0), jnp.concatenate([act, act_recv], axis=0)
        ))
        state[name] = dpre, act, swap(dpre, NEAR), swap(act, FAR)
        late[0] = dpre

    def spread_two(name):
        dpre, act, dpre_recv, act_recv = held(state[name])
        dpre_rows[name] = [dpre, dpre_recv, swap(dpre, CORE), swap(dpre_recv, CORE)]
        act_rows[name] = act, act_recv
        late[0] = dpre_recv

    def act_core(name):
        act = held(jnp.concatenate(held(act_rows[name]), axis=0))
        act_rows[name] = [act, swap(act, CORE)]
        late[0] = act

    parts = {}

    def back(name):
        part = input_part(
            dpre_rows[name], up_block, name[1] * part_width, parts.get(name[0]), marks=marks()
        )
        parts[name[0]] = part
        late[0] = part

    def q_sums():
        if q_count == 2:
            sent = held(parts["other"]).astype(jnp.bfloat16)
            parts["recv"] = swap(sent, q_masks[0])
            late[0] = sent

    def finish_rows():
        if q_count == 2:
            own, recv = held((parts["own"], parts["recv"]))
            share = own + recv.astype(jnp.float32)
        else:
            other = parts["other"].reshape(q_count - 1, rows, -1)
            share = scatter(
                jnp.concatenate([parts["own"][None], other], axis=0), q_masks[::-1]
            )[0]
        d_input = (grads_nf.astype(jnp.float32) + share).astype(jnp.bfloat16)
        saved["d_input"] = d_input
        saved["rows"] = q_pieces(d_input)
        late[0] = d_input

    def context_sums():
        gathered = jnp.concatenate(held(saved["rows"]), axis=0)
        saved["all"] = gathered
        by_order = [picked(token_source(order), gathered) for order in (NEAR_FAR, FAR_NEAR)]
        keep, send = context_parts(jnp.stack(by_order), proj_block, marks=marks())
        saved["context"] = keep, swap(send, CORE)
        late[0] = send

    def context_summed(parts, which, at):
        keep, recv, *more = parts
        columns = keep.shape[1] // 2
        here = slice(which * columns, (which + 1) * columns)
        total = keep[at, here] + recv[at, here].astype(jnp.float32)
        for part in more:
            total = total + part[which][at].astype(jnp.float32)
        return total

    def context_halved(parts, which, count):
        return context_summed(parts, which, slice(count, 2 * count)).astype(jnp.bfloat16)

    def context_core():
        parts = held(saved["context"])
        count = parts[1].shape[0] // 2
        sent = context_halved(parts, 0, count), context_halved(parts, 1, count)
        saved["context"] = *parts, (swap(sent[0], NEAR), swap(sent[1], FAR))
        late[0] = sent[0]

    def context_one():
        parts = held(saved["context"])
        count = parts[1].shape[0] // 4
        sent = context_halved(parts, 0, count), context_halved(parts, 1, count)
        saved["context"] = *parts, (swap(sent[0], FAR), swap(sent[1], NEAR))
        late[0] = sent[0]

    def context_two():
        parts = held(saved["context"])
        at = slice(0, parts[1].shape[0] // 4)
        first, second = context_summed(parts, 0, at), context_summed(parts, 1, at)
        first, second = first.astype(jnp.bfloat16), second.astype(jnp.bfloat16)
        saved["d_context"] = side_by_side(first, second, marks=marks())

    mine_a, mine_b, other_a, other_b = ("own", 0), ("own", 1), ("other", 0), ("other", 1)
    sums(mine_a)
    sums_core(mine_a)
    sums(mine_b)
    sums_one(mine_a)
    fetch(0)
    gelu(mine_a)
    spread(mine_a)
    sums_core(mine_b)
    fetch(1)
    in_all = jnp.concatenate([chunks[name][0] for name in ("own", "other")], axis=0)
    turned = in_all.T
    grad_all = jnp.concatenate([chunks[name][1] for name in ("own", "other")], axis=0)
    sums(other_a)
    sums_one(mine_b)
    spread_one(mine_a)
    gelu(mine_b)
    sums_core(other_a)
    sums(other_b)
    spread_two(mine_a)
    sums_one(other_a)
    back(mine_a)
    gelu(other_a)
    spread(other_a)
    sums_core(other_b)
    spread_one(other_a)
    sums_one(other_b)
    gelu(other_b)
    spread(other_b)
    spread_two(other_a)
    spread_one(other_b)
    back(other_a)
    spread(mine_b)
    act_core(mine_a)
    spread_two(other_b)
    spread_one(mine_b)
    context_all = lax.all_gather(held(context), "gx", axis_index_groups=groups, tiled=True)
    pieces = [piece for name in (mine_a, other_a) for piece in dpre_rows[name]]
    d_up, late[0] = up_gradient(turned, pieces, 0, width, marks=marks())
    back(other_b)
    q_sums()
    spread_two(mine_b)
    act_core(other_a)
    pieces = [piece for name in (mine_a, other_a) for piece in act_rows[name]]
    d_down, late[0] = down_gradient(pieces, grad_all, 0, width, marks=marks())
    act_core(other_b)
    act_core(mine_b)
    back(mine_b)
    finish_rows()
    pieces = [piece for name in (mine_b, other_b) for piece in dpre_rows[name]]
    d_up, late[0] = up_gradient(turned, pieces, part_width, width, d_up, marks=marks())
    pieces = [piece for name in (mine_b, other_b) for piece in act_rows[name]]
    d_down, late[0] = down_gradient(pieces, grad_all, part_width, width, d_down, marks=marks())
    context_all = held(context_all)
    context_sums()
    context_core()
    d_input_all = picked(row_of(jnp.arange(q_count * rows, dtype=jnp.int32)), saved["all"])
    d_output, late[0] = down_gradient(
        [context_all], d_input_all, 0, context_all.shape[1], marks=marks()
    )
    context_one()
    context_two()

    columns = lax.broadcasted_iota(jnp.int32, (rows, rows), 1)
    chooser = (source_nf[:, None] == columns).astype(jnp.bfloat16)
    d_input = contract(chooser, saved["d_input"], 0, 0).astype(jnp.bfloat16)

    d_context = saved["d_context"]
    return (d_input[None], d_context[None], d_up[None], d_down[None], d_output[None])


def solution(mesh):
    return jax.shard_map(
        body,
        mesh=mesh,
        in_specs=(
            P("gx", "groups", None),
            P("gx", "groups", None),
            P("gx", "groups", None),
            P("gx", None, None),
            P("gx", None, None),
            P("gx", None, None),
        ),
        out_specs=(
            P("gx", "groups", None),
            P("gx", "groups", None),
            P("gx", "groups", None),
            P("gx", "groups", None),
            P("gx", "groups", None),
        ),
        check_vma=False,
    )
```

```python
import jax
import jax.numpy as jnp
from jax import lax
from jax.experimental import pallas as pl
from jax.experimental.pallas import tpu as pltpu
from jax.sharding import PartitionSpec as P

CORE, NEAR, FAR = 1, 2, 4
SHARES = 8


def swap(value, mask):
    count = lax.axis_size("gx")
    return lax.ppermute(value, "gx", [(at, at ^ mask) for at in range(count)])


def gelu_tanh(value):
    return jax.nn.gelu(value, approximate=True)


def contract(left, right, left_dim, right_dim):
    return lax.dot_general(
        left, right, (((left_dim,), (right_dim,)), ((), ())), preferred_element_type=jnp.float32
    )


def gather(value, masks):
    for mask in masks:
        value = jnp.concatenate([value, swap(value, mask)], axis=0)
    return value


def scatter(value, masks):
    for mask in masks:
        half = value.shape[0] // 2
        sent = value[half:].astype(jnp.bfloat16)
        value = value[:half].astype(jnp.float32) + swap(sent, mask).astype(jnp.float32)
    return value


NEAR_FAR = (CORE, NEAR, FAR)
FAR_NEAR = (CORE, FAR, NEAR)


def offset_of(place, order):
    total = jnp.zeros_like(place)
    for at, mask in enumerate(order):
        total = total + mask * ((place >> (2 - at)) & 1)
    return total


def place_of(offset, order):
    total = jnp.zeros_like(offset)
    for at, mask in enumerate(order):
        total = total + jnp.where((offset & mask) != 0, 1 << (2 - at), 0)
    return total


def picked(source, value):
    columns = lax.broadcasted_iota(jnp.int32, (source.shape[0], value.shape[0]), 1)
    chooser = (source[:, None] == columns).astype(jnp.bfloat16)
    return contract(chooser, value, 1, 0).astype(jnp.bfloat16)


def turned_contract(left, right):
    if left.shape[0] % 128 or right.shape[0] % 128:
        return contract(left, right, 1, 1)
    return contract(right, left, 1, 1).T


def estimate():
    return pl.CostEstimate(flops=1, bytes_accessed=1, transcendentals=0)


def params(mebibytes):
    return pltpu.CompilerParams(
        dimension_semantics=("arbitrary",), vmem_limit_bytes=mebibytes * 1024 * 1024
    )


def tile_of(size, most):
    return most if size % most == 0 else size


def whole_block(part):
    return pl.BlockSpec(part.shape, lambda at: (0,) * part.ndim)


def run(kernel, operands, in_specs, out_specs, out_shape, grid, name, marks, aliases=None, scratch=(), memory=36):
    count = len(operands)

    def body_of(*refs):
        kernel(*refs[:count], *refs[count + len(marks) :])

    return pl.pallas_call(
        body_of,
        grid=grid,
        in_specs=list(in_specs) + [pl.BlockSpec(memory_space=pl.ANY)] * len(marks),
        out_specs=out_specs,
        out_shape=out_shape,
        input_output_aliases=aliases or {},
        scratch_shapes=scratch,
        compiler_params=params(memory),
        cost_estimate=estimate(),
        name=name,
    )(*operands, *marks)


def hidden_parts(rows_in, rows_grad, up_block, down_block, first, width, *, marks):
    count, depth = rows_in.shape
    tile = tile_of(width, 2048)
    skip = first // tile
    half = count // 2

    def kernel(in_ref, grad_ref, up_ref, down_ref, keep_ref, send_ref):
        pre = jnp.dot(in_ref[...], up_ref[...], preferred_element_type=jnp.float32)
        keep_ref[0] = pre[:half]
        send_ref[0] = pre[half:].astype(jnp.bfloat16)
        hidden = turned_contract(grad_ref[...], down_ref[...])
        keep_ref[1] = hidden[:half]
        send_ref[1] = hidden[half:].astype(jnp.bfloat16)

    return run(
        kernel,
        (rows_in, rows_grad, up_block, down_block),
        [
            whole_block(rows_in),
            whole_block(rows_grad),
            pl.BlockSpec((depth, tile), lambda at: (0, at + skip)),
            pl.BlockSpec((tile, depth), lambda at: (at + skip, 0)),
        ],
        [pl.BlockSpec((2, half, tile), lambda at: (0, 0, at))] * 2,
        (
            jax.ShapeDtypeStruct((2, half, width), jnp.float32),
            jax.ShapeDtypeStruct((2, half, width), jnp.bfloat16),
        ),
        (width // tile,),
        "hidden_parts",
        marks,
    )


def joined(pieces):
    if pieces[0].shape[0] % 16:
        return [jnp.concatenate(pieces, axis=0)]
    return pieces


def input_part(pieces, up_block, first, start=None, *, marks):
    pieces = joined(pieces)
    count = sum(piece.shape[0] for piece in pieces)
    depth = up_block.shape[0]
    width = pieces[0].shape[1]
    tile = tile_of(width, 2048)
    skip = first // tile
    begin = [] if start is None else [start]

    last = width // tile - 1
    turned = count % 128 == 0

    def kernel(*refs):
        up_ref, out_ref = refs[len(pieces)], refs[-2]
        total_ref = refs[-1]
        rows = jnp.concatenate([ref[...] for ref in refs[: len(pieces)]], axis=0)
        part = contract(up_ref[...], rows, 1, 1) if turned else contract(rows, up_ref[...], 1, 1)

        @pl.when(pl.program_id(0) == 0)
        def _():
            total_ref[...] = part

        @pl.when(pl.program_id(0) != 0)
        def _():
            total_ref[...] += part

        @pl.when(pl.program_id(0) == last)
        def _():
            total = total_ref[...].T if turned else total_ref[...]
            out_ref[...] = total + refs[-3][...] if begin else total

    result = jax.ShapeDtypeStruct((count, depth), jnp.float32)
    return run(
        kernel,
        (*pieces, up_block, *begin),
        [pl.BlockSpec((piece.shape[0], tile), lambda at: (0, at)) for piece in pieces]
        + [pl.BlockSpec((depth, tile), lambda at: (0, at + skip))]
        + [whole_block(part) for part in begin],
        whole_block(result),
        result,
        (width // tile,),
        "input_part",
        marks,
        memory=36,
        scratch=[pltpu.VMEM((depth, count) if turned else (count, depth), jnp.float32)],
    )


def up_gradient(turned, pieces, first, full, before=None, *, marks):
    pieces = joined(pieces)
    depth = turned.shape[0]
    width = pieces[0].shape[1]
    tile = tile_of(width, 2048)
    skip = first // tile
    begin = [] if before is None else [before]

    def kernel(turned_ref, *refs):
        rows = jnp.concatenate([ref[...] for ref in refs[: len(pieces)]], axis=0)
        refs[-1][...] = jnp.zeros_like(refs[-1])
        refs[-2][...] = jnp.dot(
            turned_ref[...], rows, preferred_element_type=jnp.float32
        ).astype(jnp.bfloat16)

    mark = jax.ShapeDtypeStruct((8, 128), jnp.float32)
    return run(
        kernel,
        (turned, *pieces, *begin),
        [whole_block(turned)]
        + [pl.BlockSpec((piece.shape[0], tile), lambda at: (0, at)) for piece in pieces]
        + [pl.BlockSpec(memory_space=pl.ANY)] * len(begin),
        (pl.BlockSpec((depth, tile), lambda at: (0, at + skip)), whole_block(mark)),
        (jax.ShapeDtypeStruct((depth, full), jnp.bfloat16), mark),
        (width // tile,),
        "up_gradient",
        marks,
        {1 + len(pieces): 0} if begin else {},
        memory=62,
    )


def down_gradient(pieces, rows_grad, first, full, before=None, *, marks):
    pieces = joined(pieces)
    depth = rows_grad.shape[1]
    width = pieces[0].shape[1]
    tile = tile_of(width, 2048)
    skip = first // tile
    begin = [] if before is None else [before]

    def kernel(grad_ref, *refs):
        rows = jnp.concatenate([ref[...] for ref in refs[: len(pieces)]], axis=0)
        refs[-1][...] = jnp.zeros_like(refs[-1])
        refs[-2][...] = contract(rows, grad_ref[...], 0, 0).astype(jnp.bfloat16)

    mark = jax.ShapeDtypeStruct((8, 128), jnp.float32)
    return run(
        kernel,
        (rows_grad, *pieces, *begin),
        [whole_block(rows_grad)]
        + [pl.BlockSpec((piece.shape[0], tile), lambda at: (0, at)) for piece in pieces]
        + [pl.BlockSpec(memory_space=pl.ANY)] * len(begin),
        (pl.BlockSpec((tile, depth), lambda at: (at + skip, 0)), whole_block(mark)),
        (jax.ShapeDtypeStruct((full, depth), jnp.bfloat16), mark),
        (width // tile,),
        "down_gradient",
        marks,
        {1 + len(pieces): 0} if begin else {},
        memory=36,
    )


def context_parts(rows_by_order, proj_block, *, marks):
    _, count, depth = rows_by_order.shape
    width = proj_block.shape[0]
    tile = tile_of(width // 2, 2048)
    each = width // 2 // tile
    half = count // 2

    def kernel(rows_ref, proj_ref, keep_ref, send_ref):
        part = turned_contract(rows_ref[0], proj_ref[...])
        keep_ref[...] = part[:half]
        send_ref[...] = part[half:].astype(jnp.bfloat16)

    return run(
        kernel,
        (rows_by_order, proj_block),
        [
            pl.BlockSpec((1, count, depth), lambda at: (at // each, 0, 0)),
            pl.BlockSpec((tile, depth), lambda at: (at, 0)),
        ],
        [pl.BlockSpec((half, tile), lambda at: (0, at))] * 2,
        (
            jax.ShapeDtypeStruct((half, width), jnp.float32),
            jax.ShapeDtypeStruct((half, width), jnp.bfloat16),
        ),
        (width // tile,),
        "context_parts",
        marks,
        memory=62,
    )


def side_by_side(first, second, *, marks):
    count, width = first.shape

    def kernel(first_ref, second_ref, out_ref):
        out_ref[:, :width] = first_ref[...]
        out_ref[:, width:] = second_ref[...]

    result = jax.ShapeDtypeStruct((count, 2 * width), first.dtype)
    return run(
        kernel,
        (first, second),
        [whole_block(first), whole_block(second)],
        whole_block(result),
        result,
        (1,),
        "side_by_side",
        marks,
    )


def body(input_tiles, grad_tiles, context_tiles, up_tiles, down_tiles, output_tiles):
    grid_index = lax.axis_index("gx")
    total_bits = lax.axis_size("gx").bit_length() - 1
    q_masks = [1 << bit for bit in range(3, total_bits)]
    own_p = grid_index & (SHARES - 1)
    own_q = grid_index >> 3
    inputs = input_tiles[0]
    grads = grad_tiles[0]
    context = context_tiles[0]
    up_block = up_tiles[0]
    down_block = down_tiles[0]
    proj_block = output_tiles[0]
    rows = inputs.shape[0]
    share_rows = rows // SHARES
    block_rows = context.shape[0]
    q_count = 1 << len(q_masks)
    width = up_block.shape[1]
    part_width = width // 2

    def row_source(order):
        at = jnp.arange(rows, dtype=jnp.int32)
        share = own_p ^ offset_of(at // share_rows, order)
        return share * share_rows + at % share_rows

    def row_of(token):
        local = token % rows
        place = place_of(own_p ^ (local // share_rows), NEAR_FAR)
        return ((token // rows) ^ own_q) * rows + place * share_rows + local % share_rows

    def token_source(order):
        at = jnp.arange(SHARES * block_rows, dtype=jnp.int32)
        block = own_p ^ offset_of(at // block_rows, order)
        return row_of(block * block_rows + at % block_rows)

    def q_pieces(value):
        pieces = [value]
        for mask in q_masks:
            pieces = pieces + [swap(jnp.concatenate(pieces, axis=0), mask)]
        return pieces

    def q_gather(value):
        value = value[None]
        for mask in q_masks:
            value = jnp.concatenate([value, swap(value, mask)], axis=0)
        return value

    source_nf = row_source(NEAR_FAR)
    own_rows = picked(source_nf, inputs), picked(row_source(FAR_NEAR), grads)
    pairs = [q_gather(part)[1:] for part in own_rows]
    groups = [
        [at + low for at in range(SHARES)] for low in range(0, lax.axis_size("gx"), SHARES)
    ]
    chunks = {"own": own_rows}
    grads_nf = picked(source_nf, grads)

    state, saved = {}, {}
    act_rows, dpre_rows = {}, {}
    late, alive = [own_rows[1]], []

    def corner(part):
        return part.reshape(-1, part.shape[-1])[:8, :128]

    def held(values):
        values, after = lax.optimization_barrier((values, corner(late[0])))
        alive.append(after)
        return values

    def marks():
        used = [*alive, corner(late[0])]
        alive.clear()
        return used

    def fetch(which):
        pairs[which] = held(pairs[which])
        late[0] = pairs[which]
        if which == 1:
            chunks["other"] = tuple(part.reshape((q_count - 1) * rows, -1) for part in pairs)

    def sums(name):
        chunk_in, chunk_grad = chunks[name[0]]
        keep, send = hidden_parts(
            chunk_in, chunk_grad, up_block, down_block, name[1] * part_width, part_width,
            marks=marks(),
        )
        state[name] = keep, swap(send, CORE)
        late[0] = send

    def summed(parts, which, at):
        keep, recv, *more = parts
        total = keep[which, at] + recv[which, at].astype(jnp.float32)
        for part in more:
            total = total + part[which][at].astype(jnp.float32)
        return total

    def halved(parts, which):
        count = parts[-1][which].shape[0] // 2
        return summed(parts, which, slice(count, 2 * count)).astype(jnp.bfloat16)

    def sums_core(name):
        parts = held(state[name])
        send = halved(parts, 0), halved(parts, 1)
        state[name] = *parts, (swap(send[0], NEAR), swap(send[1], FAR))
        late[0] = send[0]

    def sums_one(name):
        parts = held(state[name])
        send = halved(parts, 0), halved(parts, 1)
        state[name] = *parts, (swap(send[0], FAR), swap(send[1], NEAR))
        late[0] = send[0]

    def gelu(name):
        parts = held(state[name])
        at = slice(0, parts[-1][0].shape[0])
        act, gelu_back = jax.vjp(gelu_tanh, summed(parts, 0, at))
        dpre = gelu_back(summed(parts, 1, at))[0].astype(jnp.bfloat16)
        act = act.astype(jnp.bfloat16)
        state[name] = dpre, act
        late[0] = dpre

    def spread(name):
        dpre, act = held(state[name])
        state[name] = dpre, act, swap(dpre, FAR), swap(act, NEAR)

    def spread_one(name):
        dpre, act, dpre_recv, act_recv = held(state[name])
        dpre, act = held((
            jnp.concatenate([dpre, dpre_recv], axis=0), jnp.concatenate([act, act_recv], axis=0)
        ))
        state[name] = dpre, act, swap(dpre, NEAR), swap(act, FAR)
        late[0] = dpre

    def spread_two(name):
        dpre, act, dpre_recv, act_recv = held(state[name])
        dpre_rows[name] = [dpre, dpre_recv, swap(dpre, CORE), swap(dpre_recv, CORE)]
        act_rows[name] = act, act_recv
        late[0] = dpre_recv

    def act_core(name):
        act = held(jnp.concatenate(held(act_rows[name]), axis=0))
        act_rows[name] = [act, swap(act, CORE)]
        late[0] = act

    parts = {}

    def back(name):
        part = input_part(
            dpre_rows[name], up_block, name[1] * part_width, parts.get(name[0]), marks=marks()
        )
        parts[name[0]] = part
        late[0] = part

    def q_sums():
        if q_count == 2:
            sent = held(parts["other"]).astype(jnp.bfloat16)
            parts["recv"] = swap(sent, q_masks[0])
            late[0] = sent

    def finish_rows():
        if q_count == 2:
            own, recv = held((parts["own"], parts["recv"]))
            share = own + recv.astype(jnp.float32)
        else:
            other = parts["other"].reshape(q_count - 1, rows, -1)
            share = scatter(
                jnp.concatenate([parts["own"][None], other], axis=0), q_masks[::-1]
            )[0]
        d_input = (grads_nf.astype(jnp.float32) + share).astype(jnp.bfloat16)
        saved["d_input"] = d_input
        saved["rows"] = q_pieces(d_input)
        late[0] = d_input

    def context_sums():
        gathered = held(jnp.concatenate(held(saved["rows"]), axis=0))
        saved["all"] = gathered
        source = jnp.concatenate([token_source(NEAR_FAR), token_source(FAR_NEAR)])
        by_order = picked(source, gathered).reshape(2, *gathered.shape)
        keep, send = context_parts(by_order, proj_block, marks=marks())
        saved["context"] = keep, swap(send, CORE)
        late[0] = send

    def context_summed(parts, which, at):
        keep, recv, *more = parts
        columns = keep.shape[1] // 2
        here = slice(which * columns, (which + 1) * columns)
        total = keep[at, here] + recv[at, here].astype(jnp.float32)
        for part in more:
            total = total + part[which][at].astype(jnp.float32)
        return total

    def context_halved(parts, which, count):
        return context_summed(parts, which, slice(count, 2 * count)).astype(jnp.bfloat16)

    def context_core():
        parts = held(saved["context"])
        count = parts[1].shape[0] // 2
        sent = context_halved(parts, 0, count), context_halved(parts, 1, count)
        saved["context"] = *parts, (swap(sent[0], NEAR), swap(sent[1], FAR))
        late[0] = sent[0]

    def context_one():
        parts = held(saved["context"])
        count = parts[1].shape[0] // 4
        sent = context_halved(parts, 0, count), context_halved(parts, 1, count)
        saved["context"] = *parts, (swap(sent[0], FAR), swap(sent[1], NEAR))
        late[0] = sent[0]

    def context_two():
        parts = held(saved["context"])
        at = slice(0, parts[1].shape[0] // 4)
        first, second = context_summed(parts, 0, at), context_summed(parts, 1, at)
        first, second = first.astype(jnp.bfloat16), second.astype(jnp.bfloat16)
        saved["d_context"] = side_by_side(first, second, marks=marks())

    mine_a, mine_b, other_a, other_b = ("own", 0), ("own", 1), ("other", 0), ("other", 1)
    sums(mine_a)
    sums_core(mine_a)
    sums(mine_b)
    sums_one(mine_a)
    fetch(0)
    gelu(mine_a)
    spread(mine_a)
    sums_core(mine_b)
    fetch(1)
    in_all = jnp.concatenate([chunks[name][0] for name in ("own", "other")], axis=0)
    turned = in_all.T
    grad_all = jnp.concatenate([chunks[name][1] for name in ("own", "other")], axis=0)
    sums(other_a)
    sums_one(mine_b)
    spread_one(mine_a)
    gelu(mine_b)
    sums_core(other_a)
    sums(other_b)
    spread_two(mine_a)
    sums_one(other_a)
    back(mine_a)
    gelu(other_a)
    spread(other_a)
    sums_core(other_b)
    spread_one(other_a)
    sums_one(other_b)
    gelu(other_b)
    spread(other_b)
    spread_two(other_a)
    spread_one(other_b)
    back(other_a)
    spread(mine_b)
    act_core(mine_a)
    spread_two(other_b)
    spread_one(mine_b)
    context_all = lax.all_gather(held(context), "gx", axis_index_groups=groups, tiled=True)
    pieces = [piece for name in (mine_a, other_a) for piece in dpre_rows[name]]
    d_up, late[0] = up_gradient(turned, pieces, 0, width, marks=marks())
    back(other_b)
    q_sums()
    spread_two(mine_b)
    act_core(other_a)
    pieces = [piece for name in (mine_a, other_a) for piece in act_rows[name]]
    d_down, late[0] = down_gradient(pieces, grad_all, 0, width, marks=marks())
    act_core(other_b)
    act_core(mine_b)
    back(mine_b)
    finish_rows()
    pieces = [piece for name in (mine_b, other_b) for piece in dpre_rows[name]]
    d_up, late[0] = up_gradient(turned, pieces, part_width, width, d_up, marks=marks())
    pieces = [piece for name in (mine_b, other_b) for piece in act_rows[name]]
    d_down, late[0] = down_gradient(pieces, grad_all, part_width, width, d_down, marks=marks())
    context_all = held(context_all)
    context_sums()
    context_core()
    d_input_all = picked(row_of(jnp.arange(q_count * rows, dtype=jnp.int32)), saved["all"])
    d_output, late[0] = down_gradient(
        [context_all], d_input_all, 0, context_all.shape[1], marks=marks()
    )
    context_one()
    context_two()

    columns = lax.broadcasted_iota(jnp.int32, (rows, rows), 1)
    chooser = (source_nf[:, None] == columns).astype(jnp.bfloat16)
    d_input = contract(chooser, saved["d_input"], 0, 0).astype(jnp.bfloat16)

    d_context = saved["d_context"]
    return (d_input[None], d_context[None], d_up[None], d_down[None], d_output[None])


def solution(mesh):
    return jax.shard_map(
        body,
        mesh=mesh,
        in_specs=(
            P("gx", "groups", None),
            P("gx", "groups", None),
            P("gx", "groups", None),
            P("gx", None, None),
            P("gx", None, None),
            P("gx", None, None),
        ),
        out_specs=(
            P("gx", "groups", None),
            P("gx", "groups", None),
            P("gx", "groups", None),
            P("gx", "groups", None),
            P("gx", "groups", None),
        ),
        check_vma=False,
    )
```
